256 devices in a mesh: row: 8 (over y, z_lo), col: 32 (over z_hi, x, core).
Axes of the slice: x: 4, y: 4, z: 8 (z_hi: 4, z_lo: 2; z = z_hi * 2 + z_lo), core: 2. Of those that a mesh axis runs over, the one named last changes fastest.
Arguments:
- object_field: float32 [2, 2048, 8192], P(None, 'row', 'col'), may hold values from -6 to 6
- probe_field: float32 [2, 256, 256], replicated, may hold values from -4.2 to 4.2
- amplitudes: bfloat16 [8, 32, 6, 256, 256], P('row', 'col'), may hold values from 0 to 2
- offsets: int32 [8, 32, 6, 2], P('row', 'col'), may hold values from 0 to 256
- counts: int32 [8, 32], P('row', 'col'), may hold values from 2 to 6
Outputs:
- updated_object: float32 [2, 2048, 8192], P(None, 'row', 'col')
The draws below stay inside these ranges and needn't reach their ends.
Inputs may be any that keep to these rules, and one draw needn't show every extreme that they name: offsets[r, c, k] places slot k of tile (r, c) as stated in the reference program, so a patch reaches at most 128 pixels beyond its tile. Tile (r, c) uses slots 0 to counts[r, c] - 1; offsets and amplitudes of the other slots are ignored.
All inputs are finite; a program needn't handle non-finite values.
Results may differ from the reference program's by a relative error of at most 0.0021.
Values sent between devices are 32-bit elements; how exact they have to be, the bound alone decides.
No kernel may reach another device: no remote copies, remote signals or barrier semaphores. Data moves between devices by JAX's collectives and lax.ppermute only.
A program may use at most 64 MiB of HBM per device.

```python
import math
import jax
import jax.numpy as jnp
from jax import lax

TILE = 256
RIM = 128
MAXPOS = 6
ITERS = 2
TILES_R = 8
TILES_C = 32


def place_ends(entries, key, low, top_value):
    longest = entries.shape.index(max(entries.shape))
    spots = []
    for shift in (0, 1):
        where = [jax.random.randint(jax.random.fold_in(key, axis), (), 0, length) for axis, length in enumerate(entries.shape)]
        where[longest] = (where[longest] + shift) % entries.shape[longest]
        spots.append(tuple(where))
    return entries.at[spots[0]].set(low).at[spots[1]].set(top_value)


def steps_of(key, dims, split, least, high):
    loudness = 1.0
    for axis_at, parts in split:
        steps = jax.random.uniform(jax.random.fold_in(jax.random.fold_in(key, 6), axis_at), (parts,), jnp.float32, least / len(split), high / len(split))
        loudness = loudness * jnp.repeat(jnp.exp(steps), dims[axis_at] // parts).reshape((-1,) + (1,) * (len(dims) - 1 - axis_at))
    return loudness


def bell_draw(own_key, extent, scale, limit, cuts=(), kind=jnp.bfloat16):
    factor_of = steps_of(own_key, extent, cuts, -0.22, 0.18) if cuts else 1.0
    drawn = jax.random.normal(own_key, extent, jnp.float32) * scale * factor_of
    return jnp.minimum(jnp.maximum(drawn, -limit), limit).astype(kind)


def setup_inputs(seed: int = 0) -> dict:
    arg_keys = jax.random.split(jax.random.key(seed), 6)
    return {
        "object_field": bell_draw(arg_keys[0], (2, TILES_R * TILE, TILES_C * TILE), 1.0, 6.0, ((1, 8), (2, 32)), jnp.float32),
        "probe_field": bell_draw(arg_keys[1], (2, TILE, TILE), 0.7, 4.2, (), jnp.float32),
        "amplitudes": jnp.clip(2.0 * jax.random.uniform(arg_keys[2], (TILES_R, TILES_C, MAXPOS, TILE, TILE), jnp.float32) ** steps_of(arg_keys[2], (TILES_R, TILES_C, MAXPOS, TILE, TILE), ((0, 8), (1, 32)), -0.2, 0.2), 0.0, 2.0).astype(jnp.bfloat16),
        "offsets": place_ends(jax.random.randint(arg_keys[3], (TILES_R, TILES_C, MAXPOS, 2), 0, TILE + 1), jax.random.fold_in(arg_keys[3], 1), 0, TILE).astype(jnp.int32),
        "counts": place_ends(jax.random.randint(arg_keys[4], (TILES_R, TILES_C), 2, MAXPOS + 1), jax.random.fold_in(arg_keys[4], 1), 2, MAXPOS).astype(jnp.int32),
    }


smooth_term = 0.25
step_size = 0.5
regular_term = 1.0

def dft_table(length):
    positions = jnp.arange(length, dtype=jnp.int32)
    phase_step = positions[:, None] * positions[None, :] % length
    phase_angle = phase_step.astype(jnp.float32) * (2.0 * math.pi / length)
    norm_scale = 1.0 / math.sqrt(length)
    cosine = jnp.cos(phase_angle) * norm_scale
    sine_part = jnp.sin(phase_angle) * norm_scale
    return jnp.stack([jnp.stack([cosine, sine_part]), jnp.stack([-sine_part, cosine])]).astype(jnp.bfloat16)

def transform(field, matrices, inverse):
    if inverse:
        first_form = 'pqab,spbc->sqac'
        second_form = 'spab,pqbc->sqac'
    else:
        first_form = 'qpab,spbc->sqac'
        second_form = 'spab,qpbc->sqac'
    wide_table = matrices.astype(jnp.float32)
    half_done = jnp.einsum(first_form, wide_table, field.astype(jnp.float32), precision=lax.Precision.HIGHEST).astype(jnp.bfloat16)
    return jnp.einsum(second_form, half_done.astype(jnp.float32), wide_table, precision=lax.Precision.HIGHEST)

def patch_gradients(patches, probe_field, amplitudes, in_use, matrices):
    probe_real = probe_field[0]
    probe_imag = probe_field[1]
    object_real = patches[:, 0]
    object_imag = patches[:, 1]
    exit_wave = jnp.stack([probe_real * object_real - probe_imag * object_imag, probe_real * object_imag + probe_imag * object_real], axis=1).astype(jnp.bfloat16)
    spectrum = transform(exit_wave, matrices, False)
    modulus = jnp.sqrt(spectrum[:, 0] * spectrum[:, 0] + spectrum[:, 1] * spectrum[:, 1] + smooth_term)
    factor = (1.0 - amplitudes.astype(jnp.float32) / modulus) * in_use[:, None, None]
    residual = (spectrum * factor[:, None]).astype(jnp.bfloat16)
    back_wave = transform(residual, matrices, True)
    return jnp.stack([probe_real * back_wave[:, 0] + probe_imag * back_wave[:, 1], probe_real * back_wave[:, 1] - probe_imag * back_wave[:, 0]], axis=1)

def reference(object_field, probe_field, amplitudes, offsets, counts):
    matrices = dft_table(TILE)
    tile_total = TILES_R * TILES_C
    flat_offsets = offsets.reshape(tile_total, MAXPOS, 2)
    flat_counts = counts.reshape(tile_total)
    flat_amps = amplitudes.reshape(tile_total, MAXPOS, TILE, TILE)
    slot_index = jnp.arange(MAXPOS, dtype=jnp.int32)
    probe_power = probe_field[0] * probe_field[0] + probe_field[1] * probe_field[1]
    padded_rows = TILES_R * TILE + 2 * RIM
    padded_cols = TILES_C * TILE + 2 * RIM
    zero_index = jnp.zeros((), jnp.int32)
    tile_ids = jnp.arange(tile_total, dtype=jnp.int32)

    def corners(tile_id):
        tile_row = tile_id // TILES_C
        tile_col = tile_id % TILES_C
        top_rows = (tile_row * TILE + flat_offsets[tile_id, :, 0]).astype(jnp.int32)
        left_cols = (tile_col * TILE + flat_offsets[tile_id, :, 1]).astype(jnp.int32)
        in_use = (slot_index < flat_counts[tile_id]).astype(jnp.float32)
        return (top_rows, left_cols, in_use)

    def light_step(grid, tile_id):
        top_rows, left_cols, in_use = corners(tile_id)

        def add_light(slot, inner):
            window = lax.dynamic_slice(inner, (top_rows[slot], left_cols[slot]), (TILE, TILE))
            return lax.dynamic_update_slice(inner, window + probe_power * in_use[slot], (top_rows[slot], left_cols[slot]))
        return (lax.fori_loop(0, MAXPOS, add_light, grid), None)
    light_grid, leftover = lax.scan(light_step, jnp.zeros((padded_rows, padded_cols), jnp.float32), tile_ids)
    illumination = light_grid[RIM:RIM + TILES_R * TILE, RIM:RIM + TILES_C * TILE]
    for iteration in range(ITERS):
        padded_object = jnp.pad(object_field, ((0, 0), (RIM, RIM), (RIM, RIM)))

        def grad_step(grid, tile_id):
            top_rows, left_cols, in_use = corners(tile_id)

            def cut_patch(top_row, left_col):
                return lax.dynamic_slice(padded_object, (zero_index, top_row, left_col), (2, TILE, TILE))
            patches = jax.vmap(cut_patch)(top_rows, left_cols)
            pieces = patch_gradients(patches, probe_field, flat_amps[tile_id], in_use, matrices)

            def add_piece(slot, inner):
                where_to = (zero_index, top_rows[slot], left_cols[slot])
                window = lax.dynamic_slice(inner, where_to, (2, TILE, TILE))
                return lax.dynamic_update_slice(inner, window + pieces[slot], where_to)
            return (lax.fori_loop(0, MAXPOS, add_piece, grid), None)
        grad_grid, leftover = lax.scan(grad_step, jnp.zeros((2, padded_rows, padded_cols), jnp.float32), tile_ids)
        gradient = grad_grid[:, RIM:RIM + TILES_R * TILE, RIM:RIM + TILES_C * TILE]
        object_field = object_field - step_size * gradient / (illumination + regular_term)
    return object_field
```

```python
import functools
import math

import jax
import jax.numpy as jnp
import numpy as np
from jax import lax
from jax.experimental import pallas as pl
from jax.experimental.pallas import tpu as pltpu
from jax.sharding import PartitionSpec as P

TILE = 256
RIM = 128
MAXPOS = 6
EXT = TILE + 2 * RIM
LANES = 128
META = 16

smooth_term = 0.25
step_size = 0.5
regular_term = 1.0

VMEM = pl.BlockSpec(memory_space=pltpu.VMEM)
SMEM = pl.BlockSpec(memory_space=pltpu.SMEM)
PARAMS = pltpu.CompilerParams(vmem_limit_bytes=40 * 1024 * 1024)


def dft_tables():
    index = np.arange(TILE)
    angle = (index[:, None] * index[None, :] % TILE) * (2.0 * math.pi / TILE)
    cosine = np.cos(angle) / math.sqrt(TILE)
    sine = -np.sin(angle) / math.sqrt(TILE)
    ahead = np.block([[cosine, -sine], [sine, cosine]]).astype(np.float32)
    return jnp.asarray(ahead, jnp.bfloat16), jnp.asarray(ahead.T, jnp.bfloat16)


def swap(value, axis, first):
    count = lax.axis_size(axis)
    pairs = []
    for low in range(first, count - 1, 2):
        pairs += [(low, low + 1), (low + 1, low)]
    return lax.ppermute(value, axis, pairs)


def call(body, out_shapes, in_specs, scratch=(), flops=0, bytes_accessed=1 << 20, out_specs=None):
    return pl.pallas_call(
        body,
        out_shape=out_shapes,
        in_specs=in_specs,
        out_specs=out_specs if out_specs is not None else jax.tree.map(lambda _: VMEM, out_shapes),
        scratch_shapes=scratch,
        compiler_params=PARAMS,
        cost_estimate=pl.CostEstimate(flops=flops, bytes_accessed=bytes_accessed, transcendentals=0),
    )


def f32(*shape):
    return jax.ShapeDtypeStruct(shape, jnp.float32)


def aligned(value, unit):
    return pl.multiple_of(value, unit)


def pack_rows_kernel(place, obj, offs, cnt, a_out, b_out):
    parity = place[0] & 1
    a_row = aligned((1 - parity) * RIM, RIM)
    b_row = aligned(parity * RIM, RIM)
    for p in range(2):
        a_out[p * RIM : (p + 1) * RIM, :] = obj[p, pl.ds(a_row, RIM), :]
        b_out[p * RIM : (p + 1) * RIM, :] = obj[p, pl.ds(b_row, RIM), :]
    for out in (a_out, b_out):
        out[2 * RIM :, :] = jnp.zeros((8, TILE), jnp.float32)
        out[2 * RIM : 2 * RIM + 1, 0:12] = offs[...].astype(jnp.float32)
        out[2 * RIM : 2 * RIM + 1, 12:13] = cnt[...].astype(jnp.float32)


def pack_cols_kernel(place, obj, row_a, row_b, offs, cnt, center, a_out, b_out):
    row_parity = place[0] & 1
    a_at = aligned((1 - row_parity) * (RIM + TILE), RIM)
    b_at = aligned(row_parity * (RIM + TILE), RIM)
    for p in range(2):
        center[p, RIM : RIM + TILE, :] = obj[p]
        center[p, pl.ds(a_at, RIM), :] = row_a[p * RIM : (p + 1) * RIM, :]
        center[p, pl.ds(b_at, RIM), :] = row_b[p * RIM : (p + 1) * RIM, :]
    even = (place[1] & 1) == 0
    for p in range(2):
        low = center[p, :, 0:LANES]
        high = center[p, :, LANES:TILE]
        a_out[p * EXT : (p + 1) * EXT, :] = jnp.where(even, high, low)
        b_out[p * EXT : (p + 1) * EXT, :] = jnp.where(even, low, high)
    meta_a = row_a[2 * RIM : 2 * RIM + 1, 0:LANES]
    meta_b = row_b[2 * RIM : 2 * RIM + 1, 0:LANES]
    odd_row = row_parity == 1
    for out in (a_out, b_out):
        out[2 * EXT :, :] = jnp.zeros((8, LANES), jnp.float32)
        out[2 * EXT : 2 * EXT + 1, :] = jnp.where(odd_row, meta_a, meta_b)
        out[2 * EXT + 1 : 2 * EXT + 2, 0:12] = offs[...].astype(jnp.float32)
        out[2 * EXT + 1 : 2 * EXT + 2, 12:13] = cnt[...].astype(jnp.float32)
        out[2 * EXT + 2 : 2 * EXT + 3, :] = jnp.where(odd_row, meta_b, meta_a)


def light_kernel(metas, probe, out, canvas, padded):
    power = probe[0] * probe[0] + probe[1] * probe[1]
    padded[...] = jnp.zeros_like(padded)
    for b in range(2):
        padded[b + 1] = power[:, b * LANES : (b + 1) * LANES]
    canvas[...] = jnp.zeros_like(canvas)
    lane = lax.broadcasted_iota(jnp.int32, (TILE, LANES), 1)

    def add(index, carry):
        near = index // MAXPOS
        slot = index - near * MAXPOS
        used = slot < metas[near, 2 * MAXPOS]
        row = (near // 3) * TILE + metas[near, 2 * slot]
        col = (near % 3 - 1) * TILE - RIM + metas[near, 2 * slot + 1]
        for b in range(2):
            start = b * LANES - col

            @pl.when(used & (start > -LANES) & (start < TILE))
            def _():
                spot = start + LANES
                block = spot // LANES
                shift = spot - block * LANES
                back = (LANES - shift) & (LANES - 1)
                first = pltpu.roll(padded[block], back, 1)
                second = pltpu.roll(padded[block + 1], back, 1)
                part = jnp.where(lane < LANES - shift, first, second)
                canvas[b, pl.ds(row, TILE), :] += part

        return carry

    lax.fori_loop(0, 9 * MAXPOS, add, 0)
    for b in range(2):
        out[:, b * LANES : (b + 1) * LANES] = step_size / (
            canvas[b, TILE : TILE + EXT, :] + regular_term
        )


def iterate_kernel(
    place, offs, cnt, center, col_a, col_b, probe, amps, ahead, back, own, a_out, b_out, ext, grad, wave
):
    parity = place[1] & 1
    a_block = 3 * (1 - parity)
    b_block = 3 * parity
    for p in range(2):
        ext[p, a_block, 0:EXT, :] = col_a[p * EXT : (p + 1) * EXT, :]
        ext[p, b_block, 0:EXT, :] = col_b[p * EXT : (p + 1) * EXT, :]
        for b in range(2):
            ext[p, 1 + b, 0:EXT, :] = center[p, :, b * LANES : (b + 1) * LANES]
    grad[...] = jnp.zeros_like(grad)
    lane = lax.broadcasted_iota(jnp.int32, (TILE, LANES), 1)

    def one(slot, carry):
        row = offs[2 * slot]
        col = offs[2 * slot + 1]
        block = col // LANES
        shift = col - block * LANES
        unshift = (LANES - shift) & (LANES - 1)
        blocks = [block, block + 1, jnp.minimum(block + 2, 3)]
        keep = lane < LANES - shift
        window = []
        for p in range(2):
            turned = [pltpu.roll(ext[p, b, pl.ds(row, TILE), :], unshift, 1) for b in blocks]
            window.append([jnp.where(keep, turned[h], turned[h + 1]) for h in range(2)])
        for h in range(2):
            at = slice(h * LANES, (h + 1) * LANES)
            pr = probe[0, :, at]
            pi = probe[1, :, at]
            re = window[0][h]
            im = window[1][h]
            wave[0:TILE, at] = (pr * re - pi * im).astype(jnp.bfloat16)
            wave[TILE : 2 * TILE, at] = (pr * im + pi * re).astype(jnp.bfloat16)
        half = jnp.dot(ahead[...], wave[...], preferred_element_type=jnp.float32).astype(jnp.bfloat16)
        spectrum = jnp.dot(half[:TILE], back[0:TILE, :], preferred_element_type=jnp.float32) + jnp.dot(
            half[TILE:], back[TILE:, :], preferred_element_type=jnp.float32
        )
        sr = spectrum[:, :TILE]
        si = spectrum[:, TILE:]
        factor = 1.0 - amps[slot].astype(jnp.float32) * lax.rsqrt(sr * sr + si * si + smooth_term)
        wave[0:TILE, :] = (sr * factor).astype(jnp.bfloat16)
        wave[TILE : 2 * TILE, :] = (si * factor).astype(jnp.bfloat16)
        back_half = jnp.dot(back[...], wave[...], preferred_element_type=jnp.float32).astype(jnp.bfloat16)
        back_wave = jnp.dot(back_half[:TILE], ahead[0:TILE, :], preferred_element_type=jnp.float32) + jnp.dot(
            back_half[TILE:], ahead[TILE:, :], preferred_element_type=jnp.float32
        )
        pieces = [[], []]
        for h in range(2):
            at = slice(h * LANES, (h + 1) * LANES)
            pr = probe[0, :, at]
            pi = probe[1, :, at]
            br = back_wave[:, h * LANES : (h + 1) * LANES]
            bi = back_wave[:, TILE + h * LANES : TILE + (h + 1) * LANES]
            pieces[0].append(pltpu.roll(pr * br + pi * bi, shift, 1))
            pieces[1].append(pltpu.roll(pr * bi - pi * br, shift, 1))
        right = lane >= shift
        for p in range(2):
            h0, h1 = pieces[p]
            grad[p, blocks[0], pl.ds(row, TILE), :] += jnp.where(right, h0, 0.0)
            grad[p, blocks[1], pl.ds(row, TILE), :] += jnp.where(right, h1, h0)
            grad[p, blocks[2], pl.ds(row, TILE), :] += jnp.where(right, 0.0, h1)
        return carry

    lax.fori_loop(0, cnt[0], one, 0)
    for p in range(2):
        a_out[p * EXT : (p + 1) * EXT, :] = grad[p, a_block, 0:EXT, :]
        b_out[p * EXT : (p + 1) * EXT, :] = grad[p, b_block, 0:EXT, :]
        for b in range(2):
            own[p, :, b * LANES : (b + 1) * LANES] = grad[p, 1 + b, 0:EXT, :]


def add_cols(place, own, col_a, col_b, p):
    even = (place[1] & 1) == 0
    from_a = col_a[p * EXT : (p + 1) * EXT, :]
    from_b = col_b[p * EXT : (p + 1) * EXT, :]
    low = own[p, :, 0:LANES] + jnp.where(even, from_b, from_a)
    high = own[p, :, LANES:TILE] + jnp.where(even, from_a, from_b)
    return low, high


def fold_cols_kernel(depth, place, own, col_a, col_b, total, a_out, b_out):
    row_parity = place[0] & 1
    a_at = aligned((1 - row_parity) * (EXT - depth), RIM)
    b_at = aligned(row_parity * (EXT - depth), RIM)
    for p in range(2):
        low, high = add_cols(place, own, col_a, col_b, p)
        total[p, :, 0:LANES] = low
        total[p, :, LANES:TILE] = high
        a_out[p] = total[p, pl.ds(a_at, depth), :]
        b_out[p] = total[p, pl.ds(b_at, depth), :]


def update_wide_kernel(place, center, total, row_a, row_b, scale, fresh, a_out, b_out):
    row_parity = place[0] & 1
    a_at = aligned((1 - row_parity) * TILE, RIM)
    b_at = aligned(row_parity * TILE, RIM)
    even = (place[1] & 1) == 0
    for p in range(2):
        fresh[p, pl.ds(a_at, TILE), :] = center[p, pl.ds(a_at, TILE), :] - scale[pl.ds(a_at, TILE), :] * (
            total[p, pl.ds(a_at, TILE), :] + row_a[p]
        )
        fresh[p, pl.ds(b_at, TILE), :] = center[p, pl.ds(b_at, TILE), :] - scale[pl.ds(b_at, TILE), :] * (
            total[p, pl.ds(b_at, TILE), :] + row_b[p]
        )

    @pl.when(place[0] == 0)
    def _():
        fresh[:, 0:RIM, :] = jnp.zeros((2, RIM, TILE), jnp.float32)

    @pl.when(place[0] == place[2] - 1)
    def _():
        fresh[:, EXT - RIM :, :] = jnp.zeros((2, RIM, TILE), jnp.float32)

    for p in range(2):
        low = fresh[p, :, 0:LANES]
        high = fresh[p, :, LANES:TILE]
        a_out[p * EXT : (p + 1) * EXT, :] = jnp.where(even, high, low)
        b_out[p * EXT : (p + 1) * EXT, :] = jnp.where(even, low, high)


def update_own_kernel(place, center, total, row_a, row_b, scale, out):
    odd = (place[0] & 1) == 1
    for p in range(2):
        top = jnp.where(odd, row_a[p], row_b[p])
        bottom = jnp.where(odd, row_b[p], row_a[p])
        for half, came in ((0, top), (1, bottom)):
            at = slice(RIM + half * RIM, RIM + (half + 1) * RIM)
            out[p, half * RIM : (half + 1) * RIM, :] = center[p, at, :] - scale[at, :] * (
                total[p, at, :] + came
            )


def swaps(values, axis):
    return tuple(swap(value, axis, first) for first, value in enumerate(values))


def per_device(object_field, probe_field, amplitudes, offsets, counts):
    ahead, back = dft_tables()
    place = jnp.stack(
        [lax.axis_index("row"), lax.axis_index("col"), lax.axis_size("row"), lax.axis_size("col")]
    ).astype(jnp.int32)
    offs = offsets.reshape(1, 2 * MAXPOS)
    cnt = counts.reshape(1, 1)
    flat_offs = offsets.reshape(2 * MAXPOS)
    flat_cnt = counts.reshape(1)
    amps = amplitudes.reshape(MAXPOS, TILE, TILE)

    row_strip = f32(2 * RIM + 8, TILE)
    strips = call(pack_rows_kernel, (row_strip, row_strip), [SMEM, VMEM, VMEM, VMEM])(
        place, object_field, offs, cnt
    )
    row_a, row_b = swaps(strips, "row")
    col_strip = f32(2 * EXT + 8, LANES)
    center, a, b = call(
        pack_cols_kernel, (f32(2, EXT, TILE), col_strip, col_strip), [SMEM] + [VMEM] * 5
    )(place, object_field, row_a, row_b, offs, cnt)
    col_a, col_b = swaps((a, b), "col")

    odd = lax.axis_index("col") % 2 == 1
    near = [s[2 * EXT : 2 * EXT + 3, :META] for s in (col_a, col_b, a)]
    metas = jnp.stack(
        [jnp.where(odd, near[0], near[1]), near[2], jnp.where(odd, near[1], near[0])], axis=1
    ).reshape(9, META).astype(jnp.int32)
    scale = call(
        light_kernel,
        f32(EXT, TILE),
        [SMEM, VMEM],
        [pltpu.VMEM((2, 4 * TILE + 8, LANES), jnp.float32), pltpu.VMEM((5, TILE, LANES), jnp.float32)],
        bytes_accessed=12 << 20,
    )(metas, probe_field)

    fold_strip = f32(2 * EXT, LANES)
    iterate = call(
        iterate_kernel,
        (f32(2, EXT, TILE), fold_strip, fold_strip),
        [SMEM, SMEM, SMEM] + [VMEM] * 7,
        [
            pltpu.VMEM((2, 4, EXT + 8, LANES), jnp.float32),
            pltpu.VMEM((2, 4, EXT + 8, LANES), jnp.float32),
            pltpu.VMEM((2 * TILE, TILE), jnp.bfloat16),
        ],
        flops=3 << 30,
        bytes_accessed=6 << 20,
    )

    def fold(own, a, b, depth):
        a, b = swaps((a, b), "col")
        total, a, b = call(
            functools.partial(fold_cols_kernel, depth),
            (f32(2, EXT, TILE), f32(2, depth, TILE), f32(2, depth, TILE)),
            [SMEM] + [VMEM] * 3,
        )(place, own, a, b)
        return (total,) + swaps((a, b), "row")

    own, a, b = iterate(place, flat_offs, flat_cnt, center, col_a, col_b, probe_field, amps, ahead, back)
    total, row_a, row_b = fold(own, a, b, TILE)
    center, a, b = call(
        update_wide_kernel, (f32(2, EXT, TILE), fold_strip, fold_strip), [SMEM] + [VMEM] * 5
    )(place, center, total, row_a, row_b, scale)
    col_a, col_b = swaps((a, b), "col")
    own, a, b = iterate(place, flat_offs, flat_cnt, center, col_a, col_b, probe_field, amps, ahead, back)
    total, row_a, row_b = fold(own, a, b, RIM)
    return call(update_own_kernel, f32(2, TILE, TILE), [SMEM] + [VMEM] * 5)(
        place, center, total, row_a, row_b, scale
    )


def solution(mesh):
    in_specs = (
        P(None, "row", "col"),
        P(),
        P("row", "col", None, None, None),
        P("row", "col", None, None),
        P("row", "col"),
    )
    return jax.shard_map(
        per_device, mesh=mesh, in_specs=in_specs, out_specs=P(None, "row", "col"), check_vma=False
    )
```

```python
import functools
import math

import jax
import jax.numpy as jnp
import numpy as np
from jax import lax
from jax.experimental import pallas as pl
from jax.experimental.pallas import tpu as pltpu
from jax.sharding import PartitionSpec as P

TILE = 256
RIM = 128
MAXPOS = 6
EXT = TILE + 2 * RIM
LANES = 128

smooth_term = 0.25
step_size = 0.5
regular_term = 1.0

VMEM = pl.BlockSpec(memory_space=pltpu.VMEM)
SMEM = pl.BlockSpec(memory_space=pltpu.SMEM)


def dft_tables():
    index = np.arange(TILE)
    angle = (index[:, None] * index[None, :] % TILE) * (2.0 * math.pi / TILE)
    cosine = np.cos(angle) / math.sqrt(TILE)
    sine = -np.sin(angle) / math.sqrt(TILE)
    ahead = np.block([[cosine, -sine], [sine, cosine]]).astype(np.float32)
    return jnp.asarray(np.concatenate([ahead, ahead.T]), jnp.bfloat16)


def swap(value, axis, first):
    count = lax.axis_size(axis)
    pairs = []
    for low in range(first, count - 1, 2):
        pairs += [(low, low + 1), (low + 1, low)]
    return lax.ppermute(value, axis, pairs)


def call(body, out_shapes, in_specs, scratch=(), flops=0, bytes_accessed=1 << 20, vmem=6):
    return pl.pallas_call(
        body,
        out_shape=out_shapes,
        in_specs=in_specs,
        out_specs=jax.tree.map(lambda _: VMEM, out_shapes),
        scratch_shapes=scratch,
        compiler_params=pltpu.CompilerParams(vmem_limit_bytes=vmem << 20),
        cost_estimate=pl.CostEstimate(flops=flops, bytes_accessed=bytes_accessed, transcendentals=0),
    )


def f32(*shape):
    return pltpu.VMEM(shape, jnp.float32)


def aligned(value, unit):
    return pl.multiple_of(value, unit)


def pack_rows_kernel(place, obj, offs, cnt, a_out, b_out):
    parity = place[0] & 1
    a_row = aligned((1 - parity) * RIM, RIM)
    b_row = aligned(parity * RIM, RIM)
    for p in range(2):
        a_out[p * RIM : (p + 1) * RIM, :] = obj[p, pl.ds(a_row, RIM), :]
        b_out[p * RIM : (p + 1) * RIM, :] = obj[p, pl.ds(b_row, RIM), :]
    for out in (a_out, b_out):
        out[2 * RIM :, :] = jnp.zeros((8, TILE), jnp.float32)
        out[2 * RIM : 2 * RIM + 1, 0:12] = offs[...].astype(jnp.float32)
        out[2 * RIM : 2 * RIM + 1, 12:13] = cnt[...].astype(jnp.float32)


def pack_cols_kernel(place, obj, row_a, row_b, offs, cnt, a_out, b_out, meta):
    row_odd = place[0] & 1
    a_at = (1 - row_odd) * (RIM + TILE)
    b_at = row_odd * (RIM + TILE)
    even = (place[1] & 1) == 0
    for p in range(2):
        mine = obj[p]
        pieces = [(mine, p * EXT + RIM, TILE)]
        for row, at in ((row_a, a_at), (row_b, b_at)):
            pieces.append((row[p * RIM : (p + 1) * RIM, :], aligned(p * EXT + at, RIM), RIM))
        for piece, at, size in pieces:
            low = piece[:, 0:LANES]
            high = piece[:, LANES:TILE]
            a_out[pl.ds(at, size), :] = jnp.where(even, high, low)
            b_out[pl.ds(at, size), :] = jnp.where(even, low, high)
    meta_a = row_a[2 * RIM : 2 * RIM + 1, 0:LANES]
    meta_b = row_b[2 * RIM : 2 * RIM + 1, 0:LANES]
    odd = row_odd == 1
    meta[...] = jnp.zeros_like(meta)
    meta[0:1, :] = jnp.where(odd, meta_a, meta_b)
    meta[1:2, 0:12] = offs[...].astype(jnp.float32)
    meta[1:2, 12:13] = cnt[...].astype(jnp.float32)
    meta[2:3, :] = jnp.where(odd, meta_b, meta_a)
    a_out[2 * EXT :, :] = meta[...]
    b_out[2 * EXT :, :] = meta[...]


def center_kernel(place, obj, row_a, row_b, center):
    row_odd = place[0] & 1
    a_at = aligned((1 - row_odd) * (RIM + TILE), RIM)
    b_at = aligned(row_odd * (RIM + TILE), RIM)
    for p in range(2):
        center[p, RIM : RIM + TILE, :] = obj[p]
        center[p, pl.ds(a_at, RIM), :] = row_a[p * RIM : (p + 1) * RIM, :]
        center[p, pl.ds(b_at, RIM), :] = row_b[p * RIM : (p + 1) * RIM, :]


def light_kernel(metas, probe, out, canvas, padded):
    power = probe[0] * probe[0] + probe[1] * probe[1]
    padded[...] = jnp.zeros_like(padded)
    for b in range(2):
        padded[b + 1] = power[:, b * LANES : (b + 1) * LANES]
    canvas[...] = jnp.zeros_like(canvas)
    lane = lax.broadcasted_iota(jnp.int32, (TILE, LANES), 1)

    def add(index, carry):
        near = index // MAXPOS
        slot = index - near * MAXPOS
        where = (near % 3) * 8 + near // 3
        used = slot < metas[where, 2 * MAXPOS]
        row = (near // 3) * TILE + metas[where, 2 * slot]
        col = (near % 3 - 1) * TILE - RIM + metas[where, 2 * slot + 1]
        for b in range(2):
            start = b * LANES - col

            @pl.when(used & (start > -LANES) & (start < TILE))
            def _():
                spot = start + LANES
                block = spot // LANES
                shift = spot - block * LANES
                back = (LANES - shift) & (LANES - 1)
                first = pltpu.roll(padded[block], back, 1)
                second = pltpu.roll(padded[block + 1], back, 1)
                part = jnp.where(lane < LANES - shift, first, second)
                canvas[b, pl.ds(row, TILE), :] += part

        return carry

    lax.fori_loop(0, 9 * MAXPOS, add, 0)
    for b in range(2):
        out[:, b * LANES : (b + 1) * LANES] = step_size / (
            canvas[b, TILE : TILE + EXT, :] + regular_term
        )


def product(left, right):
    return jnp.dot(left, right, preferred_element_type=jnp.float32)


def transform(table, other, wave):
    half = product(table[...], wave).astype(jnp.bfloat16)
    return product(half[:TILE], other[0:TILE, :]) + product(half[TILE:], other[TILE:, :])


def iterate_kernel(
    first, place, offs, cnt, meta, center, col_a, col_b, probe, amps, tables, own, a_out, b_out, *rest
):
    ext, grad, wave, residual = rest[-4:]
    ahead = tables.at[0 : 2 * TILE]
    back = tables.at[2 * TILE : 4 * TILE]
    if first:
        odd = (place[1] & 1) == 1
        from_a = col_a[2 * EXT :, :]
        from_b = col_b[2 * EXT :, :]
        for side, rows in enumerate((jnp.where(odd, from_a, from_b), meta[...], jnp.where(odd, from_b, from_a))):
            rest[0][8 * side : 8 * side + 8, :] = rows.astype(jnp.int32)
    parity = place[1] & 1
    a_block = 3 * (1 - parity)
    b_block = 3 * parity
    for p in range(2):
        ext[p, a_block, 0:EXT, :] = col_a[p * EXT : (p + 1) * EXT, :]
        ext[p, b_block, 0:EXT, :] = col_b[p * EXT : (p + 1) * EXT, :]
        for b in range(2):
            ext[p, 1 + b, 0:EXT, :] = center[p, :, b * LANES : (b + 1) * LANES]
    grad[...] = jnp.zeros_like(grad)
    lane = lax.broadcasted_iota(jnp.int32, (TILE, LANES), 1)
    slots = range(MAXPOS)
    rows, shifts, blocks = [], [], []
    for slot in slots:
        col = offs[2 * slot + 1]
        block = col // LANES
        rows.append(pl.ds(offs[2 * slot], TILE))
        shifts.append(col - block * LANES)
        blocks.append([block, block + 1, jnp.minimum(block + 2, 3)])
    for slot in slots:
        unshift = (LANES - shifts[slot]) & (LANES - 1)
        keep = lane < LANES - shifts[slot]
        window = []
        for p in range(2):
            turned = [pltpu.roll(ext[p, b, rows[slot], :], unshift, 1) for b in blocks[slot]]
            window.append([jnp.where(keep, turned[h], turned[h + 1]) for h in range(2)])
        for h in range(2):
            at = slice(h * LANES, (h + 1) * LANES)
            pr = probe[0, :, at]
            pi = probe[1, :, at]
            re = window[0][h]
            im = window[1][h]
            wave[slot, 0:TILE, at] = (pr * re - pi * im).astype(jnp.bfloat16)
            wave[slot, TILE : 2 * TILE, at] = (pr * im + pi * re).astype(jnp.bfloat16)
    spectra = [transform(ahead, back, wave[slot]) for slot in slots]
    for slot in slots:
        used = jnp.where(slot < cnt[0], 1.0, 0.0)
        sr = spectra[slot][:, :TILE]
        si = spectra[slot][:, TILE:]
        root = lax.rsqrt(sr * sr + si * si + smooth_term)
        factor = (1.0 - amps[slot].astype(jnp.float32) * root) * used
        residual[slot, 0:TILE, :] = (sr * factor).astype(jnp.bfloat16)
        residual[slot, TILE : 2 * TILE, :] = (si * factor).astype(jnp.bfloat16)
    waves = [transform(back, ahead, residual[slot]) for slot in slots]
    for slot in slots:
        pieces = [[], []]
        for h in range(2):
            at = slice(h * LANES, (h + 1) * LANES)
            pr = probe[0, :, at]
            pi = probe[1, :, at]
            br = waves[slot][:, h * LANES : (h + 1) * LANES]
            bi = waves[slot][:, TILE + h * LANES : TILE + (h + 1) * LANES]
            pieces[0].append(pltpu.roll(pr * br + pi * bi, shifts[slot], 1))
            pieces[1].append(pltpu.roll(pr * bi - pi * br, shifts[slot], 1))
        right = lane >= shifts[slot]
        for p in range(2):
            h0, h1 = pieces[p]
            grad[p, blocks[slot][0], rows[slot], :] += jnp.where(right, h0, 0.0)
            grad[p, blocks[slot][1], rows[slot], :] += jnp.where(right, h1, h0)
            grad[p, blocks[slot][2], rows[slot], :] += jnp.where(right, 0.0, h1)
    for p in range(2):
        a_out[p * EXT : (p + 1) * EXT, :] = grad[p, a_block, 0:EXT, :]
        b_out[p * EXT : (p + 1) * EXT, :] = grad[p, b_block, 0:EXT, :]
        for b in range(2):
            own[p, :, b * LANES : (b + 1) * LANES] = grad[p, 1 + b, 0:EXT, :]


def add_cols(place, own, col_a, col_b, p):
    even = (place[1] & 1) == 0
    from_a = col_a[p * EXT : (p + 1) * EXT, :]
    from_b = col_b[p * EXT : (p + 1) * EXT, :]
    low = own[p, :, 0:LANES] + jnp.where(even, from_b, from_a)
    high = own[p, :, LANES:TILE] + jnp.where(even, from_a, from_b)
    return low, high


def fold_cols_kernel(depth, place, own, col_a, col_b, total, a_out, b_out):
    row_parity = place[0] & 1
    a_at = aligned((1 - row_parity) * (EXT - depth), RIM)
    b_at = aligned(row_parity * (EXT - depth), RIM)
    for p in range(2):
        low, high = add_cols(place, own, col_a, col_b, p)
        total[p, :, 0:LANES] = low
        total[p, :, LANES:TILE] = high
        a_out[p] = total[p, pl.ds(a_at, depth), :]
        b_out[p] = total[p, pl.ds(b_at, depth), :]


def update_wide_kernel(place, center, total, row_a, row_b, scale, fresh, a_out, b_out):
    row_parity = place[0] & 1
    a_at = aligned((1 - row_parity) * TILE, RIM)
    b_at = aligned(row_parity * TILE, RIM)
    even = (place[1] & 1) == 0
    for p in range(2):
        fresh[p, pl.ds(a_at, TILE), :] = center[p, pl.ds(a_at, TILE), :] - scale[pl.ds(a_at, TILE), :] * (
            total[p, pl.ds(a_at, TILE), :] + row_a[p]
        )
        fresh[p, pl.ds(b_at, TILE), :] = center[p, pl.ds(b_at, TILE), :] - scale[pl.ds(b_at, TILE), :] * (
            total[p, pl.ds(b_at, TILE), :] + row_b[p]
        )

    @pl.when(place[0] == 0)
    def _():
        fresh[:, 0:RIM, :] = jnp.zeros((2, RIM, TILE), jnp.float32)

    @pl.when(place[0] == place[2] - 1)
    def _():
        fresh[:, EXT - RIM :, :] = jnp.zeros((2, RIM, TILE), jnp.float32)

    for p in range(2):
        low = fresh[p, :, 0:LANES]
        high = fresh[p, :, LANES:TILE]
        a_out[p * EXT : (p + 1) * EXT, :] = jnp.where(even, high, low)
        b_out[p * EXT : (p + 1) * EXT, :] = jnp.where(even, low, high)


def update_own_kernel(place, center, total, row_a, row_b, scale, out):
    odd = (place[0] & 1) == 1
    for p in range(2):
        top = jnp.where(odd, row_a[p], row_b[p])
        bottom = jnp.where(odd, row_b[p], row_a[p])
        for half, came in ((0, top), (1, bottom)):
            at = slice(RIM + half * RIM, RIM + (half + 1) * RIM)
            out[p, half * RIM : (half + 1) * RIM, :] = center[p, at, :] - scale[at, :] * (
                total[p, at, :] + came
            )


def swaps(values, axis):
    far = swap(values[1], axis, 1)
    return swap(values[0], axis, 0), far


def per_device(object_field, probe_field, amplitudes, offsets, counts):
    tables = dft_tables()
    place = jnp.stack(
        [lax.axis_index("row"), lax.axis_index("col"), lax.axis_size("row"), lax.axis_size("col")]
    ).astype(jnp.int32)
    offs = offsets.reshape(1, 2 * MAXPOS)
    cnt = counts.reshape(1, 1)
    flat_offs = offsets.reshape(2 * MAXPOS)
    flat_cnt = counts.reshape(1)
    amps = amplitudes.reshape(MAXPOS, TILE, TILE)

    row_strip = f32(2 * RIM + 8, TILE)
    strips = call(pack_rows_kernel, (row_strip, row_strip), [SMEM, VMEM, VMEM, VMEM])(
        place, object_field, offs, cnt
    )
    row_a, row_b = swaps(strips, "row")
    col_strip = f32(2 * EXT + 8, LANES)
    a, b, meta = call(pack_cols_kernel, (col_strip, col_strip, f32(8, LANES)), [SMEM] + [VMEM] * 5)(
        place, object_field, row_a, row_b, offs, cnt
    )
    center = call(center_kernel, f32(2, EXT, TILE), [SMEM] + [VMEM] * 3, bytes_accessed=4 << 20)(
        place, object_field, row_a, row_b
    )
    col_a, col_b = swaps((a, b), "col")

    fold_strip = f32(2 * EXT, LANES)
    grid = pltpu.VMEM((2, 4, EXT + 8, LANES), jnp.float32)
    stack = pltpu.VMEM((MAXPOS, 2 * TILE, TILE), jnp.bfloat16)

    def iterate(first, center, cols):
        outs = (f32(2, EXT, TILE), fold_strip, fold_strip)
        if first:
            outs += (jax.ShapeDtypeStruct((24, LANES), jnp.int32),)
        return call(
            functools.partial(iterate_kernel, first),
            outs,
            [SMEM] * 3 + [VMEM] * 7,
            [grid, grid, stack, stack],
            flops=3 << 30,
            bytes_accessed=6 << 20,
            vmem=14,
        )(place, flat_offs, flat_cnt, meta, center, *cols, probe_field, amps, tables)

    def fold(first, center, cols, depth):
        own, a, b, *metas = iterate(first, center, cols)
        a, b = swaps((a, b), "col")
        total, a, b = call(
            functools.partial(fold_cols_kernel, depth),
            (f32(2, EXT, TILE), f32(2, depth, TILE), f32(2, depth, TILE)),
            [SMEM] + [VMEM] * 3,
        )(place, own, a, b)
        return (total, metas) + swaps((a, b), "row")

    total, metas, row_a, row_b = fold(True, center, (col_a, col_b), TILE)
    scale = call(
        light_kernel,
        f32(EXT, TILE),
        [SMEM, VMEM],
        [pltpu.VMEM((2, 4 * TILE + 8, LANES), jnp.float32), pltpu.VMEM((5, TILE, LANES), jnp.float32)],
        bytes_accessed=12 << 20,
    )(metas[0], probe_field)
    center, a, b = call(
        update_wide_kernel, (f32(2, EXT, TILE), fold_strip, fold_strip), [SMEM] + [VMEM] * 5
    )(place, center, total, row_a, row_b, scale)
    total, _, row_a, row_b = fold(False, center, swaps((a, b), "col"), RIM)
    return call(
        update_own_kernel, jax.ShapeDtypeStruct((2, TILE, TILE), jnp.float32), [SMEM] + [VMEM] * 5
    )(place, center, total, row_a, row_b, scale)


def solution(mesh):
    in_specs = (
        P(None, "row", "col"),
        P(),
        P("row", "col", None, None, None),
        P("row", "col", None, None),
        P("row", "col"),
    )
    return jax.shard_map(
        per_device, mesh=mesh, in_specs=in_specs, out_specs=P(None, "row", "col"), check_vma=False
    )
```

```python
import functools
import math

import jax
import jax.numpy as jnp
import numpy as np
from jax import lax
from jax.experimental import pallas as pl
from jax.experimental.pallas import tpu as pltpu
from jax.sharding import PartitionSpec as P

TILE = 256
RIM = 128
MAXPOS = 6
EXT = TILE + 2 * RIM
LANES = 128

smooth_term = 0.25
step_size = 0.5
regular_term = 1.0

VMEM = pl.BlockSpec(memory_space=pltpu.VMEM)
SMEM = pl.BlockSpec(memory_space=pltpu.SMEM)


def dft_tables():
    index = np.arange(TILE)
    angle = (index[:, None] * index[None, :] % TILE) * (2.0 * math.pi / TILE)
    cosine = np.cos(angle) / math.sqrt(TILE)
    sine = -np.sin(angle) / math.sqrt(TILE)
    ahead = np.block([[cosine, -sine], [sine, cosine]]).astype(np.float32)
    return jnp.asarray(np.concatenate([ahead, ahead.T]), jnp.bfloat16)


def swap(value, axis, first):
    count = lax.axis_size(axis)
    pairs = []
    for low in range(first, count - 1, 2):
        pairs += [(low, low + 1), (low + 1, low)]
    return lax.ppermute(value, axis, pairs)


def call(body, out_shapes, in_specs, scratch=(), flops=0, bytes_accessed=1 << 20, vmem=6):
    return pl.pallas_call(
        body,
        out_shape=out_shapes,
        in_specs=in_specs,
        out_specs=jax.tree.map(lambda _: VMEM, out_shapes),
        scratch_shapes=scratch,
        compiler_params=pltpu.CompilerParams(vmem_limit_bytes=vmem << 20),
        cost_estimate=pl.CostEstimate(flops=flops, bytes_accessed=bytes_accessed, transcendentals=0),
    )


def f32(*shape):
    return pltpu.VMEM(shape, jnp.float32)


def aligned(value, unit):
    return pl.multiple_of(value, unit)


def own_meta(offs, cnt, width):
    lane = lax.broadcasted_iota(jnp.int32, (1, width), 1)
    row = jnp.where(lane == 2 * MAXPOS, cnt[0, 0], 0)
    for slot in range(MAXPOS):
        row = jnp.where(lane == 2 * slot, offs[0, slot], row)
        row = jnp.where(lane == 2 * slot + 1, offs[1, slot], row)
    return row.astype(jnp.float32)


def pack_rows_kernel(place, obj, offs, cnt, a_out, b_out, arrived):
    parity = place[0] & 1
    copies = []
    for p in range(2):
        for out, at in ((a_out, 1 - parity), (b_out, parity)):
            copies.append(
                pltpu.make_async_copy(
                    obj.at[p, pl.ds(aligned(at * RIM, RIM), RIM), :],
                    out.at[pl.ds(p * RIM, RIM), :],
                    arrived.at[len(copies)],
                )
            )
            copies[-1].start()
    meta = own_meta(offs, cnt, TILE)
    for out in (a_out, b_out):
        out[2 * RIM :, :] = jnp.zeros((8, TILE), jnp.float32)
        out[2 * RIM : 2 * RIM + 1, :] = meta
    for copy in copies:
        copy.wait()


def pack_cols_kernel(near, place, obj, row_a, row_b, offs, cnt, out, meta):
    row_odd = place[0] & 1
    a_at = (1 - row_odd) * (RIM + TILE)
    b_at = row_odd * (RIM + TILE)
    high_side = (place[1] & 1) == (0 if near else 1)
    for p in range(2):
        pieces = [(obj[p], p * EXT + RIM, TILE)]
        for row, at in ((row_a, a_at), (row_b, b_at)):
            pieces.append((row[p * RIM : (p + 1) * RIM, :], aligned(p * EXT + at, RIM), RIM))
        for piece, at, size in pieces:
            out[pl.ds(at, size), :] = jnp.where(high_side, piece[:, LANES:TILE], piece[:, 0:LANES])
    meta_a = row_a[2 * RIM : 2 * RIM + 1, 0:LANES]
    meta_b = row_b[2 * RIM : 2 * RIM + 1, 0:LANES]
    odd = row_odd == 1
    meta[...] = jnp.zeros_like(meta)
    meta[0:1, :] = jnp.where(odd, meta_a, meta_b)
    meta[1:2, :] = own_meta(offs, cnt, LANES)
    meta[2:3, :] = jnp.where(odd, meta_b, meta_a)
    out[2 * EXT :, :] = meta[...]


def center_kernel(place, obj, row_a, row_b, tables, center):
    row_odd = place[0] & 1
    a_at = aligned((1 - row_odd) * (RIM + TILE), RIM)
    b_at = aligned(row_odd * (RIM + TILE), RIM)
    for p in range(2):
        center[p, RIM : RIM + TILE, :] = obj[p]
        center[p, pl.ds(a_at, RIM), :] = row_a[p * RIM : (p + 1) * RIM, :]
        center[p, pl.ds(b_at, RIM), :] = row_b[p * RIM : (p + 1) * RIM, :]


def light_kernel(metas, probe, out, canvas, padded):
    power = probe[0] * probe[0] + probe[1] * probe[1]
    padded[...] = jnp.zeros_like(padded)
    for b in range(2):
        padded[b + 1] = power[:, b * LANES : (b + 1) * LANES]
    canvas[...] = jnp.zeros_like(canvas)
    lane = lax.broadcasted_iota(jnp.int32, (TILE, LANES), 1)

    def add(index, carry):
        near = index // MAXPOS
        slot = index - near * MAXPOS
        where = (near % 3) * 8 + near // 3
        used = slot < metas[where, 2 * MAXPOS]
        row = (near // 3) * TILE + metas[where, 2 * slot]
        col = (near % 3 - 1) * TILE - RIM + metas[where, 2 * slot + 1]
        for b in range(2):
            start = b * LANES - col

            @pl.when(used & (start > -LANES) & (start < TILE))
            def _():
                spot = start + LANES
                block = spot // LANES
                shift = spot - block * LANES
                back = (LANES - shift) & (LANES - 1)
                first = pltpu.roll(padded[block], back, 1)
                second = pltpu.roll(padded[block + 1], back, 1)
                part = jnp.where(lane < LANES - shift, first, second)
                canvas[b, pl.ds(row, TILE), :] += part

        return carry

    lax.fori_loop(0, 9 * MAXPOS, add, 0)
    for b in range(2):
        out[:, b * LANES : (b + 1) * LANES] = step_size / (
            canvas[b, TILE : TILE + EXT, :] + regular_term
        )


def product(left, right):
    return jnp.dot(left, right, preferred_element_type=jnp.float32)


def transform(table, other, wave):
    half = product(table[...], wave).astype(jnp.bfloat16)
    return product(half[:TILE], other[0:TILE, :]) + product(half[TILE:], other[TILE:, :])


def iterate_kernel(
    first, place, offs, cnt, meta, center, col_1, col_2, probe, amps, tables, own, a_out, b_out, *rest
):
    ext, grad, wave, residual = rest[-4:]
    col_a, col_b = (col_1, col_2) if first else (col_2, col_1)
    ahead = tables.at[0 : 2 * TILE]
    back = tables.at[2 * TILE : 4 * TILE]
    if first:
        odd = (place[1] & 1) == 1
        from_a = col_a[2 * EXT :, :]
        from_b = col_b[2 * EXT :, :]
        for side, rows in enumerate((jnp.where(odd, from_a, from_b), meta[...], jnp.where(odd, from_b, from_a))):
            rest[0][8 * side : 8 * side + 8, :] = rows.astype(jnp.int32)
    parity = place[1] & 1
    a_block = 3 * (1 - parity)
    b_block = 3 * parity
    for p in range(2):
        ext[p, a_block, 0:EXT, :] = col_a[p * EXT : (p + 1) * EXT, :]
        ext[p, b_block, 0:EXT, :] = col_b[p * EXT : (p + 1) * EXT, :]
        for b in range(2):
            ext[p, 1 + b, 0:EXT, :] = center[p, :, b * LANES : (b + 1) * LANES]
    grad[...] = jnp.zeros_like(grad)
    lane = lax.broadcasted_iota(jnp.int32, (TILE, LANES), 1)
    slots = range(MAXPOS)
    rows, shifts, blocks = [], [], []
    for slot in slots:
        col = offs[1, slot]
        block = col // LANES
        rows.append(pl.ds(offs[0, slot], TILE))
        shifts.append(col - block * LANES)
        blocks.append([block, block + 1, jnp.minimum(block + 2, 3)])
    for slot in slots:
        unshift = (LANES - shifts[slot]) & (LANES - 1)
        keep = lane < LANES - shifts[slot]
        window = []
        for p in range(2):
            turned = [pltpu.roll(ext[p, b, rows[slot], :], unshift, 1) for b in blocks[slot]]
            window.append([jnp.where(keep, turned[h], turned[h + 1]) for h in range(2)])
        for h in range(2):
            at = slice(h * LANES, (h + 1) * LANES)
            pr = probe[0, :, at]
            pi = probe[1, :, at]
            re = window[0][h]
            im = window[1][h]
            wave[slot, 0:TILE, at] = (pr * re - pi * im).astype(jnp.bfloat16)
            wave[slot, TILE : 2 * TILE, at] = (pr * im + pi * re).astype(jnp.bfloat16)
    spectra = [transform(ahead, back, wave[slot]) for slot in slots]
    for slot in slots:
        used = jnp.where(slot < cnt[0, 0], 1.0, 0.0)
        sr = spectra[slot][:, :TILE]
        si = spectra[slot][:, TILE:]
        root = lax.rsqrt(sr * sr + si * si + smooth_term)
        factor = (1.0 - amps[slot].astype(jnp.float32) * root) * used
        residual[slot, 0:TILE, :] = (sr * factor).astype(jnp.bfloat16)
        residual[slot, TILE : 2 * TILE, :] = (si * factor).astype(jnp.bfloat16)
    waves = [transform(back, ahead, residual[slot]) for slot in slots]
    for slot in slots:
        pieces = [[], []]
        for h in range(2):
            at = slice(h * LANES, (h + 1) * LANES)
            pr = probe[0, :, at]
            pi = probe[1, :, at]
            br = waves[slot][:, h * LANES : (h + 1) * LANES]
            bi = waves[slot][:, TILE + h * LANES : TILE + (h + 1) * LANES]
            pieces[0].append(pltpu.roll(pr * br + pi * bi, shifts[slot], 1))
            pieces[1].append(pltpu.roll(pr * bi - pi * br, shifts[slot], 1))
        right = lane >= shifts[slot]
        for p in range(2):
            h0, h1 = pieces[p]
            grad[p, blocks[slot][0], rows[slot], :] += jnp.where(right, h0, 0.0)
            grad[p, blocks[slot][1], rows[slot], :] += jnp.where(right, h1, h0)
            grad[p, blocks[slot][2], rows[slot], :] += jnp.where(right, 0.0, h1)
    for p in range(2):
        a_out[p * EXT : (p + 1) * EXT, :] = grad[p, a_block, 0:EXT, :]
        b_out[p * EXT : (p + 1) * EXT, :] = grad[p, b_block, 0:EXT, :]
        for b in range(2):
            own[p, :, b * LANES : (b + 1) * LANES] = grad[p, 1 + b, 0:EXT, :]


def add_cols(place, own, col_a, col_b, p):
    even = (place[1] & 1) == 0
    from_a = col_a[p * EXT : (p + 1) * EXT, :]
    from_b = col_b[p * EXT : (p + 1) * EXT, :]
    low = own[p, :, 0:LANES] + jnp.where(even, from_b, from_a)
    high = own[p, :, LANES:TILE] + jnp.where(even, from_a, from_b)
    return low, high


def fold_cols_kernel(depth, place, own, col_b, col_a, total, a_out, b_out):
    row_parity = place[0] & 1
    a_at = aligned((1 - row_parity) * (EXT - depth), RIM)
    b_at = aligned(row_parity * (EXT - depth), RIM)
    for p in range(2):
        low, high = add_cols(place, own, col_a, col_b, p)
        total[p, :, 0:LANES] = low
        total[p, :, LANES:TILE] = high
        a_out[p] = total[p, pl.ds(a_at, depth), :]
        b_out[p] = total[p, pl.ds(b_at, depth), :]


def update_wide_kernel(place, center, total, row_a, row_b, scale, fresh, a_out, b_out):
    row_parity = place[0] & 1
    a_at = aligned((1 - row_parity) * TILE, RIM)
    b_at = aligned(row_parity * TILE, RIM)
    even = (place[1] & 1) == 0
    for p in range(2):
        fresh[p, pl.ds(a_at, TILE), :] = center[p, pl.ds(a_at, TILE), :] - scale[pl.ds(a_at, TILE), :] * (
            total[p, pl.ds(a_at, TILE), :] + row_a[p]
        )
        fresh[p, pl.ds(b_at, TILE), :] = center[p, pl.ds(b_at, TILE), :] - scale[pl.ds(b_at, TILE), :] * (
            total[p, pl.ds(b_at, TILE), :] + row_b[p]
        )

    @pl.when(place[0] == 0)
    def _():
        fresh[:, 0:RIM, :] = jnp.zeros((2, RIM, TILE), jnp.float32)

    @pl.when(place[0] == place[2] - 1)
    def _():
        fresh[:, EXT - RIM :, :] = jnp.zeros((2, RIM, TILE), jnp.float32)

    for p in range(2):
        low = fresh[p, :, 0:LANES]
        high = fresh[p, :, LANES:TILE]
        a_out[p * EXT : (p + 1) * EXT, :] = jnp.where(even, high, low)
        b_out[p * EXT : (p + 1) * EXT, :] = jnp.where(even, low, high)


def update_own_kernel(place, center, total, row_a, row_b, scale, out, fresh, left):
    odd = (place[0] & 1) == 1
    copies = []
    for p in range(2):
        top = jnp.where(odd, row_a[p], row_b[p])
        bottom = jnp.where(odd, row_b[p], row_a[p])
        for half, came in ((0, top), (1, bottom)):
            at = slice(RIM + half * RIM, RIM + (half + 1) * RIM)
            rows = slice(half * RIM, (half + 1) * RIM)
            fresh[p, rows, :] = center[p, at, :] - scale[at, :] * (total[p, at, :] + came)
            copies.append(
                pltpu.make_async_copy(fresh.at[p, rows, :], out.at[p, rows, :], left.at[len(copies)])
            )
            copies[-1].start()
    for copy in copies:
        copy.wait()


def swaps(values, axis):
    far = swap(values[1], axis, 1)
    return swap(values[0], axis, 0), far


def per_device(object_field, probe_field, amplitudes, offsets, counts):
    tables = dft_tables()
    place = jnp.stack(
        [lax.axis_index("row"), lax.axis_index("col"), lax.axis_size("row"), lax.axis_size("col")]
    ).astype(jnp.int32)
    offs = jnp.transpose(offsets, (0, 1, 3, 2)).reshape(2, MAXPOS)
    cnt = counts.reshape(1, 1)
    amps = amplitudes.reshape(MAXPOS, TILE, TILE)

    row_strip = f32(2 * RIM + 8, TILE)
    strips = call(
        pack_rows_kernel,
        (row_strip, row_strip),
        [SMEM, pl.BlockSpec(memory_space=pl.ANY), SMEM, SMEM],
        [pltpu.SemaphoreType.DMA((4,))],
    )(place, object_field, offs, cnt)
    row_a, row_b = swaps(strips, "row")

    def pack_cols(near):
        return call(
            functools.partial(pack_cols_kernel, near),
            (f32(2 * EXT + 8, LANES), f32(8, LANES)),
            [SMEM] + [VMEM] * 3 + [SMEM] * 2,
            bytes_accessed=(8 << 20) if near else (1 << 20),
        )(place, object_field, row_a, row_b, offs, cnt)

    b, meta = pack_cols(False)
    a, _ = pack_cols(True)
    center = call(center_kernel, f32(2, EXT, TILE), [SMEM] + [VMEM] * 4, bytes_accessed=4 << 20)(
        place, object_field, row_a, row_b, tables
    )
    col_a, col_b = swaps((a, b), "col")

    fold_strip = f32(2 * EXT, LANES)
    grid = pltpu.VMEM((2, 4, EXT + 8, LANES), jnp.float32)
    stack = pltpu.VMEM((MAXPOS, 2 * TILE, TILE), jnp.bfloat16)

    def iterate(first, center, cols):
        outs = (f32(2, EXT, TILE), fold_strip, fold_strip)
        if first:
            outs += (jax.ShapeDtypeStruct((24, LANES), jnp.int32),)
        return call(
            functools.partial(iterate_kernel, first),
            outs,
            [SMEM] * 3 + [VMEM] * 7,
            [grid, grid, stack, stack],
            flops=3 << 30,
            bytes_accessed=6 << 20,
            vmem=14,
        )(place, offs, cnt, meta, center, *(cols if first else cols[::-1]), probe_field, amps, tables)

    def fold(first, center, cols, depth):
        own, a, b, *metas = iterate(first, center, cols)
        a, b = swaps((a, b), "col")
        total, a, b = call(
            functools.partial(fold_cols_kernel, depth),
            (f32(2, EXT, TILE), f32(2, depth, TILE), f32(2, depth, TILE)),
            [SMEM] + [VMEM] * 3,
        )(place, own, b, a)
        return (total, metas) + swaps((a, b), "row")

    total, metas, row_a, row_b = fold(True, center, (col_a, col_b), TILE)
    scale = call(
        light_kernel,
        f32(EXT, TILE),
        [SMEM, VMEM],
        [pltpu.VMEM((2, 4 * TILE + 8, LANES), jnp.float32), pltpu.VMEM((5, TILE, LANES), jnp.float32)],
        bytes_accessed=12 << 20,
    )(metas[0], probe_field)
    center, a, b = call(
        update_wide_kernel, (f32(2, EXT, TILE), fold_strip, fold_strip), [SMEM] + [VMEM] * 5
    )(place, center, total, row_a, row_b, scale)
    total, _, row_a, row_b = fold(False, center, swaps((a, b), "col"), RIM)
    return pl.pallas_call(
        update_own_kernel,
        out_shape=jax.ShapeDtypeStruct((2, TILE, TILE), jnp.float32),
        in_specs=[SMEM] + [VMEM] * 5,
        out_specs=pl.BlockSpec(memory_space=pl.ANY),
        scratch_shapes=[pltpu.VMEM((2, TILE, TILE), jnp.float32), pltpu.SemaphoreType.DMA((4,))],
        compiler_params=pltpu.CompilerParams(vmem_limit_bytes=6 << 20),
    )(place, center, total, row_a, row_b, scale)


def solution(mesh):
    in_specs = (
        P(None, "row", "col"),
        P(),
        P("row", "col", None, None, None),
        P("row", "col", None, None),
        P("row", "col"),
    )
    return jax.shard_map(
        per_device, mesh=mesh, in_specs=in_specs, out_specs=P(None, "row", "col"), check_vma=False
    )
```

```python
import functools
import math

import jax
import jax.numpy as jnp
import numpy as np
from jax import lax
from jax.experimental import pallas as pl
from jax.experimental.pallas import tpu as pltpu
from jax.sharding import PartitionSpec as P

TILE = 256
RIM = 128
MAXPOS = 6
EXT = TILE + 2 * RIM
LANES = 128

smooth_term = 0.25
step_size = 0.5
regular_term = 1.0

VMEM = pl.BlockSpec(memory_space=pltpu.VMEM)
SMEM = pl.BlockSpec(memory_space=pltpu.SMEM)


def dft_tables():
    index = np.arange(TILE)
    angle = (index[:, None] * index[None, :] % TILE) * (2.0 * math.pi / TILE)
    cosine = np.cos(angle) / math.sqrt(TILE)
    sine = -np.sin(angle) / math.sqrt(TILE)
    ahead = np.block([[cosine, -sine], [sine, cosine]]).astype(np.float32)
    return jnp.asarray(np.concatenate([ahead, ahead.T]), jnp.bfloat16)


def swap(value, axis, first):
    count = lax.axis_size(axis)
    pairs = []
    for low in range(first, count - 1, 2):
        pairs += [(low, low + 1), (low + 1, low)]
    return lax.ppermute(value, axis, pairs)


def call(body, out_shapes, in_specs, scratch=(), flops=0, bytes_accessed=1 << 20, vmem=6):
    return pl.pallas_call(
        body,
        out_shape=out_shapes,
        in_specs=in_specs,
        out_specs=jax.tree.map(lambda _: VMEM, out_shapes),
        scratch_shapes=scratch,
        compiler_params=pltpu.CompilerParams(vmem_limit_bytes=vmem << 20),
        cost_estimate=pl.CostEstimate(flops=flops, bytes_accessed=bytes_accessed, transcendentals=0),
    )


def f32(*shape):
    return pltpu.VMEM(shape, jnp.float32)


def aligned(value, unit):
    return pl.multiple_of(value, unit)


def pack_rows_kernel(place, obj, offs, cnt, a_out, b_out):
    parity = place[0] & 1
    a_row = aligned((1 - parity) * RIM, RIM)
    b_row = aligned(parity * RIM, RIM)
    for p in range(2):
        a_out[p * RIM : (p + 1) * RIM, :] = obj[p, pl.ds(a_row, RIM), :]
        b_out[p * RIM : (p + 1) * RIM, :] = obj[p, pl.ds(b_row, RIM), :]
    for out in (a_out, b_out):
        out[2 * RIM :, :] = jnp.zeros((8, TILE), jnp.float32)
        out[2 * RIM : 2 * RIM + 1, 0:12] = offs[...].astype(jnp.float32)
        out[2 * RIM : 2 * RIM + 1, 12:13] = cnt[...].astype(jnp.float32)


def pack_cols_kernel(near, place, obj, row_a, row_b, offs, cnt, out, *meta_out):
    row_odd = place[0] & 1
    a_at = (1 - row_odd) * (RIM + TILE)
    b_at = row_odd * (RIM + TILE)
    high_side = (place[1] & 1) == (0 if near else 1)
    for p in range(2):
        pieces = [(obj[p], p * EXT + RIM, TILE)]
        for row, at in ((row_a, a_at), (row_b, b_at)):
            pieces.append((row[p * RIM : (p + 1) * RIM, :], aligned(p * EXT + at, RIM), RIM))
        for piece, at, size in pieces:
            out[pl.ds(at, size), :] = jnp.where(high_side, piece[:, LANES:TILE], piece[:, 0:LANES])
    meta_a = row_a[2 * RIM : 2 * RIM + 1, 0:LANES]
    meta_b = row_b[2 * RIM : 2 * RIM + 1, 0:LANES]
    odd = row_odd == 1
    meta = out.at[2 * EXT :, :]
    meta[...] = jnp.zeros((8, LANES), jnp.float32)
    meta[0:1, :] = jnp.where(odd, meta_a, meta_b)
    meta[1:2, 0:12] = offs[...].astype(jnp.float32)
    meta[1:2, 12:13] = cnt[...].astype(jnp.float32)
    meta[2:3, :] = jnp.where(odd, meta_b, meta_a)
    for more in meta_out:
        more[...] = meta[...]


def center_kernel(place, obj, row_a, row_b, tables, center):
    row_odd = place[0] & 1
    a_at = aligned((1 - row_odd) * (RIM + TILE), RIM)
    b_at = aligned(row_odd * (RIM + TILE), RIM)
    for p in range(2):
        center[p, RIM : RIM + TILE, :] = obj[p]
        center[p, pl.ds(a_at, RIM), :] = row_a[p * RIM : (p + 1) * RIM, :]
        center[p, pl.ds(b_at, RIM), :] = row_b[p * RIM : (p + 1) * RIM, :]


def light_kernel(metas, probe, out, canvas, padded):
    power = probe[0] * probe[0] + probe[1] * probe[1]
    padded[...] = jnp.zeros_like(padded)
    for b in range(2):
        padded[b + 1] = power[:, b * LANES : (b + 1) * LANES]
    canvas[...] = jnp.zeros_like(canvas)
    lane = lax.broadcasted_iota(jnp.int32, (TILE, LANES), 1)

    def add(index, carry):
        near = index // MAXPOS
        slot = index - near * MAXPOS
        where = (near % 3) * 8 + near // 3
        used = slot < metas[where, 2 * MAXPOS]
        row = (near // 3) * TILE + metas[where, 2 * slot]
        col = (near % 3 - 1) * TILE - RIM + metas[where, 2 * slot + 1]
        for b in range(2):
            start = b * LANES - col

            @pl.when(used & (start > -LANES) & (start < TILE))
            def _():
                spot = start + LANES
                block = spot // LANES
                shift = spot - block * LANES
                back = (LANES - shift) & (LANES - 1)
                first = pltpu.roll(padded[block], back, 1)
                second = pltpu.roll(padded[block + 1], back, 1)
                part = jnp.where(lane < LANES - shift, first, second)
                canvas[b, pl.ds(row, TILE), :] += part

        return carry

    lax.fori_loop(0, 9 * MAXPOS, add, 0)
    for b in range(2):
        out[:, b * LANES : (b + 1) * LANES] = step_size / (
            canvas[b, TILE : TILE + EXT, :] + regular_term
        )


def product(left, right):
    return jnp.dot(left, right, preferred_element_type=jnp.float32)


def transform(table, other, wave):
    half = product(table[...], wave).astype(jnp.bfloat16)
    return product(half[:TILE], other[0:TILE, :]) + product(half[TILE:], other[TILE:, :])


def iterate_kernel(
    first, place, offs, cnt, meta, center, col_a, col_b, probe, amps, tables, own, a_out, b_out, *rest
):
    ext, grad, wave, residual = rest[-4:]
    ahead = tables.at[0 : 2 * TILE]
    back = tables.at[2 * TILE : 4 * TILE]
    if first:
        odd = (place[1] & 1) == 1
        from_a = col_a[2 * EXT :, :]
        from_b = col_b[2 * EXT :, :]
        for side, rows in enumerate((jnp.where(odd, from_a, from_b), meta[...], jnp.where(odd, from_b, from_a))):
            rest[0][8 * side : 8 * side + 8, :] = rows.astype(jnp.int32)
    parity = place[1] & 1
    a_block = 3 * (1 - parity)
    b_block = 3 * parity
    for p in range(2):
        ext[p, a_block, 0:EXT, :] = col_a[p * EXT : (p + 1) * EXT, :]
        ext[p, b_block, 0:EXT, :] = col_b[p * EXT : (p + 1) * EXT, :]
        for b in range(2):
            ext[p, 1 + b, 0:EXT, :] = center[p, :, b * LANES : (b + 1) * LANES]
    grad[...] = jnp.zeros_like(grad)
    lane = lax.broadcasted_iota(jnp.int32, (TILE, LANES), 1)
    slots = range(MAXPOS)
    rows, shifts, blocks = [], [], []
    for slot in slots:
        in_use = slot < cnt[0]
        col = jnp.where(in_use, offs[2 * slot + 1], 0)
        block = col // LANES
        rows.append(pl.ds(jnp.where(in_use, offs[2 * slot], 0), TILE))
        shifts.append(col - block * LANES)
        blocks.append([block, block + 1, jnp.minimum(block + 2, 3)])
    for slot in slots:
        unshift = (LANES - shifts[slot]) & (LANES - 1)
        keep = lane < LANES - shifts[slot]
        window = []
        for p in range(2):
            turned = [pltpu.roll(ext[p, b, rows[slot], :], unshift, 1) for b in blocks[slot]]
            window.append([jnp.where(keep, turned[h], turned[h + 1]) for h in range(2)])
        for h in range(2):
            at = slice(h * LANES, (h + 1) * LANES)
            pr = probe[0, :, at]
            pi = probe[1, :, at]
            re = window[0][h]
            im = window[1][h]
            wave[slot, 0:TILE, at] = (pr * re - pi * im).astype(jnp.bfloat16)
            wave[slot, TILE : 2 * TILE, at] = (pr * im + pi * re).astype(jnp.bfloat16)
    spectra = [transform(ahead, back, wave[slot]) for slot in slots]
    for slot in slots:
        used = jnp.where(slot < cnt[0], 1.0, 0.0)
        sr = spectra[slot][:, :TILE]
        si = spectra[slot][:, TILE:]
        root = lax.rsqrt(sr * sr + si * si + smooth_term)
        factor = (1.0 - amps[slot].astype(jnp.float32) * root) * used
        residual[slot, 0:TILE, :] = (sr * factor).astype(jnp.bfloat16)
        residual[slot, TILE : 2 * TILE, :] = (si * factor).astype(jnp.bfloat16)
    waves = [transform(back, ahead, residual[slot]) for slot in slots]
    for slot in slots:
        pieces = [[], []]
        for h in range(2):
            at = slice(h * LANES, (h + 1) * LANES)
            pr = probe[0, :, at]
            pi = probe[1, :, at]
            br = waves[slot][:, h * LANES : (h + 1) * LANES]
            bi = waves[slot][:, TILE + h * LANES : TILE + (h + 1) * LANES]
            pieces[0].append(pltpu.roll(pr * br + pi * bi, shifts[slot], 1))
            pieces[1].append(pltpu.roll(pr * bi - pi * br, shifts[slot], 1))
        right = lane >= shifts[slot]
        for p in range(2):
            h0, h1 = pieces[p]
            grad[p, blocks[slot][0], rows[slot], :] += jnp.where(right, h0, 0.0)
            grad[p, blocks[slot][1], rows[slot], :] += jnp.where(right, h1, h0)
            grad[p, blocks[slot][2], rows[slot], :] += jnp.where(right, 0.0, h1)
    for p in range(2):
        a_out[p * EXT : (p + 1) * EXT, :] = grad[p, a_block, 0:EXT, :]
        b_out[p * EXT : (p + 1) * EXT, :] = grad[p, b_block, 0:EXT, :]
        for b in range(2):
            own[p, :, b * LANES : (b + 1) * LANES] = grad[p, 1 + b, 0:EXT, :]


def add_cols(place, own, col_a, col_b, p):
    even = (place[1] & 1) == 0
    from_a = col_a[p * EXT : (p + 1) * EXT, :]
    from_b = col_b[p * EXT : (p + 1) * EXT, :]
    low = own[p, :, 0:LANES] + jnp.where(even, from_b, from_a)
    high = own[p, :, LANES:TILE] + jnp.where(even, from_a, from_b)
    return low, high


def fold_cols_kernel(depth, place, own, col_a, col_b, total, a_out, b_out):
    row_parity = place[0] & 1
    a_at = aligned((1 - row_parity) * (EXT - depth), RIM)
    b_at = aligned(row_parity * (EXT - depth), RIM)
    for p in range(2):
        low, high = add_cols(place, own, col_a, col_b, p)
        total[p, :, 0:LANES] = low
        total[p, :, LANES:TILE] = high
        a_out[p] = total[p, pl.ds(a_at, depth), :]
        b_out[p] = total[p, pl.ds(b_at, depth), :]


def update_wide_kernel(place, center, total, row_a, row_b, scale, fresh, a_out, b_out):
    row_parity = place[0] & 1
    a_at = aligned((1 - row_parity) * TILE, RIM)
    b_at = aligned(row_parity * TILE, RIM)
    even = (place[1] & 1) == 0
    for p in range(2):
        fresh[p, pl.ds(a_at, TILE), :] = center[p, pl.ds(a_at, TILE), :] - scale[pl.ds(a_at, TILE), :] * (
            total[p, pl.ds(a_at, TILE), :] + row_a[p]
        )
        fresh[p, pl.ds(b_at, TILE), :] = center[p, pl.ds(b_at, TILE), :] - scale[pl.ds(b_at, TILE), :] * (
            total[p, pl.ds(b_at, TILE), :] + row_b[p]
        )

    @pl.when(place[0] == 0)
    def _():
        fresh[:, 0:RIM, :] = jnp.zeros((2, RIM, TILE), jnp.float32)

    @pl.when(place[0] == place[2] - 1)
    def _():
        fresh[:, EXT - RIM :, :] = jnp.zeros((2, RIM, TILE), jnp.float32)

    for p in range(2):
        low = fresh[p, :, 0:LANES]
        high = fresh[p, :, LANES:TILE]
        a_out[p * EXT : (p + 1) * EXT, :] = jnp.where(even, high, low)
        b_out[p * EXT : (p + 1) * EXT, :] = jnp.where(even, low, high)


def update_own_kernel(place, center, total, row_a, row_b, scale, out):
    odd = (place[0] & 1) == 1
    for p in range(2):
        top = jnp.where(odd, row_a[p], row_b[p])
        bottom = jnp.where(odd, row_b[p], row_a[p])
        for half, came in ((0, top), (1, bottom)):
            at = slice(RIM + half * RIM, RIM + (half + 1) * RIM)
            out[p, half * RIM : (half + 1) * RIM, :] = center[p, at, :] - scale[at, :] * (
                total[p, at, :] + came
            )


def swaps(values, axis):
    far = swap(values[1], axis, 1)
    return swap(values[0], axis, 0), far


def per_device(object_field, probe_field, amplitudes, offsets, counts):
    tables = dft_tables()
    place = jnp.stack(
        [lax.axis_index("row"), lax.axis_index("col"), lax.axis_size("row"), lax.axis_size("col")]
    ).astype(jnp.int32)
    offs = offsets.reshape(1, 2 * MAXPOS)
    cnt = counts.reshape(1, 1)
    flat_offs = offsets.reshape(2 * MAXPOS)
    flat_cnt = counts.reshape(1)
    amps = amplitudes.reshape(MAXPOS, TILE, TILE)

    row_strip = f32(2 * RIM + 8, TILE)
    strips = call(pack_rows_kernel, (row_strip, row_strip), [SMEM, VMEM, VMEM, VMEM])(
        place, object_field, offs, cnt
    )
    row_a, row_b = swaps(strips, "row")
    col_strip = f32(2 * EXT + 8, LANES)
    def pack_cols(near, *more):
        return call(
            functools.partial(pack_cols_kernel, near), (col_strip,) + more, [SMEM] + [VMEM] * 5
        )(place, object_field, row_a, row_b, offs, cnt)

    (a,) = pack_cols(True)
    b, meta = pack_cols(False, f32(8, LANES))
    center = call(center_kernel, f32(2, EXT, TILE), [SMEM] + [VMEM] * 4, bytes_accessed=4 << 20)(
        place, object_field, row_a, row_b, tables
    )
    col_a, col_b = swaps((a, b), "col")

    fold_strip = f32(2 * EXT, LANES)
    grid = pltpu.VMEM((2, 4, EXT + 8, LANES), jnp.float32)
    stack = pltpu.VMEM((MAXPOS, 2 * TILE, TILE), jnp.bfloat16)

    def iterate(first, center, cols):
        outs = (f32(2, EXT, TILE), fold_strip, fold_strip)
        if first:
            outs += (jax.ShapeDtypeStruct((24, LANES), jnp.int32),)
        return call(
            functools.partial(iterate_kernel, first),
            outs,
            [SMEM] * 3 + [VMEM] * 7,
            [grid, grid, stack, stack],
            flops=3 << 30,
            bytes_accessed=6 << 20,
            vmem=14,
        )(place, flat_offs, flat_cnt, meta, center, *cols, probe_field, amps, tables)

    def fold(first, center, cols, depth):
        own, a, b, *metas = iterate(first, center, cols)
        a, b = swaps((a, b), "col")
        total, a, b = call(
            functools.partial(fold_cols_kernel, depth),
            (f32(2, EXT, TILE), f32(2, depth, TILE), f32(2, depth, TILE)),
            [SMEM] + [VMEM] * 3,
        )(place, own, a, b)
        return (total, metas) + swaps((a, b), "row")

    total, metas, row_a, row_b = fold(True, center, (col_a, col_b), TILE)
    scale = call(
        light_kernel,
        f32(EXT, TILE),
        [SMEM, VMEM],
        [pltpu.VMEM((2, 4 * TILE + 8, LANES), jnp.float32), pltpu.VMEM((5, TILE, LANES), jnp.float32)],
        bytes_accessed=12 << 20,
    )(metas[0], probe_field)
    center, a, b = call(
        update_wide_kernel, (f32(2, EXT, TILE), fold_strip, fold_strip), [SMEM] + [VMEM] * 5
    )(place, center, total, row_a, row_b, scale)
    total, _, row_a, row_b = fold(False, center, swaps((a, b), "col"), RIM)
    return call(
        update_own_kernel, jax.ShapeDtypeStruct((2, TILE, TILE), jnp.float32), [SMEM] + [VMEM] * 5
    )(place, center, total, row_a, row_b, scale)


def solution(mesh):
    in_specs = (
        P(None, "row", "col"),
        P(),
        P("row", "col", None, None, None),
        P("row", "col", None, None),
        P("row", "col"),
    )
    return jax.shard_map(
        per_device, mesh=mesh, in_specs=in_specs, out_specs=P(None, "row", "col"), check_vma=False
    )
```

```python
import functools
import math

import jax
import jax.numpy as jnp
import numpy as np
from jax import lax
from jax.experimental import pallas as pl
from jax.experimental.pallas import tpu as pltpu
from jax.sharding import PartitionSpec as P

TILE = 256
RIM = 128
MAXPOS = 6
EXT = TILE + 2 * RIM
LANES = 128

smooth_term = 0.25
step_size = 0.5
regular_term = 1.0

VMEM = pl.BlockSpec(memory_space=pltpu.VMEM)
SMEM = pl.BlockSpec(memory_space=pltpu.SMEM)


def dft_tables():
    index = np.arange(TILE)
    angle = (index[:, None] * index[None, :] % TILE) * (2.0 * math.pi / TILE)
    cosine = np.cos(angle) / math.sqrt(TILE)
    sine = -np.sin(angle) / math.sqrt(TILE)
    ahead = np.block([[cosine, -sine], [sine, cosine]]).astype(np.float32)
    return jnp.asarray(np.concatenate([ahead, ahead.T]), jnp.bfloat16)


def swap(value, axis, first):
    count = lax.axis_size(axis)
    pairs = []
    for low in range(first, count - 1, 2):
        pairs += [(low, low + 1), (low + 1, low)]
    return lax.ppermute(value, axis, pairs)


def call(body, out_shapes, in_specs, scratch=(), flops=0, bytes_accessed=1 << 20, vmem=6):
    return pl.pallas_call(
        body,
        out_shape=out_shapes,
        in_specs=in_specs,
        out_specs=jax.tree.map(lambda _: VMEM, out_shapes),
        scratch_shapes=scratch,
        compiler_params=pltpu.CompilerParams(vmem_limit_bytes=vmem << 20),
        cost_estimate=pl.CostEstimate(flops=flops, bytes_accessed=bytes_accessed, transcendentals=0),
    )


def f32(*shape):
    return pltpu.VMEM(shape, jnp.float32)


def aligned(value, unit):
    return pl.multiple_of(value, unit)


def pack_rows_kernel(place, obj, offs, cnt, a_out, b_out):
    parity = place[0] & 1
    a_row = aligned((1 - parity) * RIM, RIM)
    b_row = aligned(parity * RIM, RIM)
    for p in range(2):
        a_out[p * RIM : (p + 1) * RIM, :] = obj[p, pl.ds(a_row, RIM), :]
        b_out[p * RIM : (p + 1) * RIM, :] = obj[p, pl.ds(b_row, RIM), :]
    for out in (a_out, b_out):
        out[2 * RIM :, :] = jnp.zeros((8, TILE), jnp.float32)
        out[2 * RIM : 2 * RIM + 1, 0:12] = offs[...].astype(jnp.float32)
        out[2 * RIM : 2 * RIM + 1, 12:13] = cnt[...].astype(jnp.float32)


def pack_cols_kernel(near, place, obj, row_a, row_b, offs, cnt, out, *meta_out):
    row_odd = place[0] & 1
    a_at = (1 - row_odd) * (RIM + TILE)
    b_at = row_odd * (RIM + TILE)
    high_side = (place[1] & 1) == (0 if near else 1)
    for p in range(2):
        pieces = [(obj[p], p * EXT + RIM, TILE)]
        for row, at in ((row_a, a_at), (row_b, b_at)):
            pieces.append((row[p * RIM : (p + 1) * RIM, :], aligned(p * EXT + at, RIM), RIM))
        for piece, at, size in pieces:
            out[pl.ds(at, size), :] = jnp.where(high_side, piece[:, LANES:TILE], piece[:, 0:LANES])
    meta_a = row_a[2 * RIM : 2 * RIM + 1, 0:LANES]
    meta_b = row_b[2 * RIM : 2 * RIM + 1, 0:LANES]
    odd = row_odd == 1
    meta = out.at[2 * EXT :, :]
    meta[...] = jnp.zeros((8, LANES), jnp.float32)
    meta[0:1, :] = jnp.where(odd, meta_a, meta_b)
    meta[1:2, 0:12] = offs[...].astype(jnp.float32)
    meta[1:2, 12:13] = cnt[...].astype(jnp.float32)
    meta[2:3, :] = jnp.where(odd, meta_b, meta_a)
    for more in meta_out:
        more[...] = meta[...]


def center_kernel(place, obj, row_a, row_b, tables, center):
    row_odd = place[0] & 1
    a_at = aligned((1 - row_odd) * (RIM + TILE), RIM)
    b_at = aligned(row_odd * (RIM + TILE), RIM)
    for p in range(2):
        center[p, RIM : RIM + TILE, :] = obj[p]
        center[p, pl.ds(a_at, RIM), :] = row_a[p * RIM : (p + 1) * RIM, :]
        center[p, pl.ds(b_at, RIM), :] = row_b[p * RIM : (p + 1) * RIM, :]


def light_kernel(metas, probe, out, canvas, padded):
    power = probe[0] * probe[0] + probe[1] * probe[1]
    padded[...] = jnp.zeros_like(padded)
    for b in range(2):
        padded[b + 1] = power[:, b * LANES : (b + 1) * LANES]
    canvas[...] = jnp.zeros_like(canvas)
    lane = lax.broadcasted_iota(jnp.int32, (TILE, LANES), 1)

    def add(index, carry):
        near = index // MAXPOS
        slot = index - near * MAXPOS
        where = (near % 3) * 8 + near // 3
        used = slot < metas[where, 2 * MAXPOS]
        row = (near // 3) * TILE + metas[where, 2 * slot]
        col = (near % 3 - 1) * TILE - RIM + metas[where, 2 * slot + 1]
        for b in range(2):
            start = b * LANES - col

            @pl.when(used & (start > -LANES) & (start < TILE))
            def _():
                spot = start + LANES
                block = spot // LANES
                shift = spot - block * LANES
                back = (LANES - shift) & (LANES - 1)
                first = pltpu.roll(padded[block], back, 1)
                second = pltpu.roll(padded[block + 1], back, 1)
                part = jnp.where(lane < LANES - shift, first, second)
                canvas[b, pl.ds(row, TILE), :] += part

        return carry

    lax.fori_loop(0, 9 * MAXPOS, add, 0)
    for b in range(2):
        out[:, b * LANES : (b + 1) * LANES] = step_size / (
            canvas[b, TILE : TILE + EXT, :] + regular_term
        )


def product(left, right):
    return jnp.dot(left, right, preferred_element_type=jnp.float32)


def transform(table, other, wave):
    half = product(table[...], wave).astype(jnp.bfloat16)
    return product(half[:TILE], other[0:TILE, :]) + product(half[TILE:], other[TILE:, :])


def iterate_kernel(
    first, place, offs, cnt, meta, center, col_a, col_b, probe, amps, tables, own, a_out, b_out, *rest
):
    ext, grad, wave, residual = rest[-4:]
    ahead = tables.at[0 : 2 * TILE]
    back = tables.at[2 * TILE : 4 * TILE]
    if first:
        odd = (place[1] & 1) == 1
        from_a = col_a[2 * EXT :, :]
        from_b = col_b[2 * EXT :, :]
        for side, rows in enumerate((jnp.where(odd, from_a, from_b), meta[...], jnp.where(odd, from_b, from_a))):
            rest[0][8 * side : 8 * side + 8, :] = rows.astype(jnp.int32)
    parity = place[1] & 1
    a_block = 3 * (1 - parity)
    b_block = 3 * parity
    for p in range(2):
        ext[p, a_block, 0:EXT, :] = col_a[p * EXT : (p + 1) * EXT, :]
        ext[p, b_block, 0:EXT, :] = col_b[p * EXT : (p + 1) * EXT, :]
        for b in range(2):
            ext[p, 1 + b, 0:EXT, :] = center[p, :, b * LANES : (b + 1) * LANES]
    grad[...] = jnp.zeros_like(grad)
    lane = lax.broadcasted_iota(jnp.int32, (TILE, LANES), 1)
    slots = range(MAXPOS)
    rows, shifts, blocks = [], [], []
    for slot in slots:
        in_use = slot < cnt[0]
        col = jnp.where(in_use, offs[2 * slot + 1], 0)
        block = col // LANES
        rows.append(pl.ds(jnp.where(in_use, offs[2 * slot], 0), TILE))
        shifts.append(col - block * LANES)
        blocks.append([block, block + 1, jnp.minimum(block + 2, 3)])
    for slot in slots:
        unshift = (LANES - shifts[slot]) & (LANES - 1)
        keep = lane < LANES - shifts[slot]
        window = []
        for p in range(2):
            turned = [pltpu.roll(ext[p, b, rows[slot], :], unshift, 1) for b in blocks[slot]]
            window.append([jnp.where(keep, turned[h], turned[h + 1]) for h in range(2)])
        for h in range(2):
            at = slice(h * LANES, (h + 1) * LANES)
            pr = probe[0, :, at]
            pi = probe[1, :, at]
            re = window[0][h]
            im = window[1][h]
            wave[slot, 0:TILE, at] = (pr * re - pi * im).astype(jnp.bfloat16)
            wave[slot, TILE : 2 * TILE, at] = (pr * im + pi * re).astype(jnp.bfloat16)
    spectra = [transform(ahead, back, wave[slot]) for slot in slots]
    for slot in slots:
        used = jnp.where(slot < cnt[0], 1.0, 0.0)
        sr = spectra[slot][:, :TILE]
        si = spectra[slot][:, TILE:]
        root = lax.rsqrt(sr * sr + si * si + smooth_term)
        factor = (1.0 - amps[slot].astype(jnp.float32) * root) * used
        residual[slot, 0:TILE, :] = (sr * factor).astype(jnp.bfloat16)
        residual[slot, TILE : 2 * TILE, :] = (si * factor).astype(jnp.bfloat16)
    waves = [transform(back, ahead, residual[slot]) for slot in slots]
    for slot in slots:
        pieces = [[], []]
        for h in range(2):
            at = slice(h * LANES, (h + 1) * LANES)
            pr = probe[0, :, at]
            pi = probe[1, :, at]
            br = waves[slot][:, h * LANES : (h + 1) * LANES]
            bi = waves[slot][:, TILE + h * LANES : TILE + (h + 1) * LANES]
            pieces[0].append(pltpu.roll(pr * br + pi * bi, shifts[slot], 1))
            pieces[1].append(pltpu.roll(pr * bi - pi * br, shifts[slot], 1))
        right = lane >= shifts[slot]
        for p in range(2):
            h0, h1 = pieces[p]
            grad[p, blocks[slot][0], rows[slot], :] += jnp.where(right, h0, 0.0)
            grad[p, blocks[slot][1], rows[slot], :] += jnp.where(right, h1, h0)
            grad[p, blocks[slot][2], rows[slot], :] += jnp.where(right, 0.0, h1)
    for p in range(2):
        a_out[p * EXT : (p + 1) * EXT, :] = grad[p, a_block, 0:EXT, :]
        b_out[p * EXT : (p + 1) * EXT, :] = grad[p, b_block, 0:EXT, :]
        for b in range(2):
            own[p, :, b * LANES : (b + 1) * LANES] = grad[p, 1 + b, 0:EXT, :]


def by_side(place, from_a, from_b):
    even = (place[1] & 1) == 0
    return jnp.where(even, from_b, from_a), jnp.where(even, from_a, from_b)


def fold_strips_kernel(depth, place, own, col_a, col_b, a_out, b_out):
    row_parity = place[0] & 1
    for out, end in ((a_out, 1 - row_parity), (b_out, row_parity)):
        at = end * (EXT - depth)
        mine = pl.ds(aligned(at, RIM), depth)
        for p in range(2):
            theirs = pl.ds(aligned(p * EXT + at, RIM), depth)
            left, right = by_side(place, col_a[theirs, :], col_b[theirs, :])
            out[p, :, 0:LANES] = own[p, mine, 0:LANES] + left
            out[p, :, LANES:TILE] = own[p, mine, LANES:TILE] + right


def fold_inner_kernel(place, own, col_a, col_b, total):
    mine = slice(RIM, RIM + TILE)
    for p in range(2):
        theirs = slice(p * EXT + RIM, p * EXT + RIM + TILE)
        left, right = by_side(place, col_a[theirs, :], col_b[theirs, :])
        total[p, :, 0:LANES] = own[p, mine, 0:LANES] + left
        total[p, :, LANES:TILE] = own[p, mine, LANES:TILE] + right


def update_wide_kernel(place, center, sent_a, sent_b, row_a, row_b, scale, fresh, a_out, b_out):
    row_parity = place[0] & 1
    even = (place[1] & 1) == 0
    for sent, came, end in ((sent_a, row_a, 1 - row_parity), (sent_b, row_b, row_parity)):
        rows = pl.ds(aligned(end * TILE, RIM), TILE)
        for p in range(2):
            fresh[p, rows, :] = center[p, rows, :] - scale[rows, :] * (sent[p] + came[p])

    @pl.when(place[0] == 0)
    def _():
        fresh[:, 0:RIM, :] = jnp.zeros((2, RIM, TILE), jnp.float32)

    @pl.when(place[0] == place[2] - 1)
    def _():
        fresh[:, EXT - RIM :, :] = jnp.zeros((2, RIM, TILE), jnp.float32)

    for p in range(2):
        low = fresh[p, :, 0:LANES]
        high = fresh[p, :, LANES:TILE]
        a_out[p * EXT : (p + 1) * EXT, :] = jnp.where(even, high, low)
        b_out[p * EXT : (p + 1) * EXT, :] = jnp.where(even, low, high)


def update_own_kernel(place, center, total, row_a, row_b, scale, out):
    odd = (place[0] & 1) == 1
    for p in range(2):
        top = jnp.where(odd, row_a[p], row_b[p])
        bottom = jnp.where(odd, row_b[p], row_a[p])
        for half, came in ((0, top), (1, bottom)):
            at = slice(RIM + half * RIM, RIM + (half + 1) * RIM)
            out[p, half * RIM : (half + 1) * RIM, :] = center[p, at, :] - scale[at, :] * (
                total[p, half * RIM : (half + 1) * RIM, :] + came
            )


def swaps(values, axis):
    far = swap(values[1], axis, 1)
    return swap(values[0], axis, 0), far


def per_device(object_field, probe_field, amplitudes, offsets, counts):
    tables = dft_tables()
    place = jnp.stack(
        [lax.axis_index("row"), lax.axis_index("col"), lax.axis_size("row"), lax.axis_size("col")]
    ).astype(jnp.int32)
    offs = offsets.reshape(1, 2 * MAXPOS)
    cnt = counts.reshape(1, 1)
    flat_offs = offsets.reshape(2 * MAXPOS)
    flat_cnt = counts.reshape(1)
    amps = amplitudes.reshape(MAXPOS, TILE, TILE)

    row_strip = f32(2 * RIM + 8, TILE)
    strips = call(pack_rows_kernel, (row_strip, row_strip), [SMEM, VMEM, VMEM, VMEM])(
        place, object_field, offs, cnt
    )
    row_a, row_b = swaps(strips, "row")
    col_strip = f32(2 * EXT + 8, LANES)
    def pack_cols(near, *more):
        return call(
            functools.partial(pack_cols_kernel, near), (col_strip,) + more, [SMEM] + [VMEM] * 5
        )(place, object_field, row_a, row_b, offs, cnt)

    (a,) = pack_cols(True)
    b, meta = pack_cols(False, f32(8, LANES))
    center = call(center_kernel, f32(2, EXT, TILE), [SMEM] + [VMEM] * 4, bytes_accessed=4 << 20)(
        place, object_field, row_a, row_b, tables
    )
    col_a, col_b = swaps((a, b), "col")

    fold_strip = f32(2 * EXT, LANES)
    grid = pltpu.VMEM((2, 4, EXT + 8, LANES), jnp.float32)
    stack = pltpu.VMEM((MAXPOS, 2 * TILE, TILE), jnp.bfloat16)

    def iterate(first, center, cols):
        outs = (f32(2, EXT, TILE), fold_strip, fold_strip)
        if first:
            outs += (jax.ShapeDtypeStruct((24, LANES), jnp.int32),)
        return call(
            functools.partial(iterate_kernel, first),
            outs,
            [SMEM] * 3 + [VMEM] * 7,
            [grid, grid, stack, stack],
            flops=3 << 30,
            bytes_accessed=6 << 20,
            vmem=14,
        )(place, flat_offs, flat_cnt, meta, center, *cols, probe_field, amps, tables)

    def fold(first, center, cols, depth):
        own, a, b, *metas = iterate(first, center, cols)
        a, b = swaps((a, b), "col")
        sent = call(
            functools.partial(fold_strips_kernel, depth),
            (f32(2, depth, TILE), f32(2, depth, TILE)),
            [SMEM] + [VMEM] * 3,
        )(place, own, a, b)
        came = swaps(sent, "row")
        if first:
            return sent, metas[0], came
        total = call(fold_inner_kernel, f32(2, TILE, TILE), [SMEM] + [VMEM] * 3, bytes_accessed=4 << 20)(
            place, own, a, b
        )
        return total, None, came

    sent, metas, came = fold(True, center, (col_a, col_b), TILE)
    scale = call(
        light_kernel,
        f32(EXT, TILE),
        [SMEM, VMEM],
        [pltpu.VMEM((2, 4 * TILE + 8, LANES), jnp.float32), pltpu.VMEM((5, TILE, LANES), jnp.float32)],
        bytes_accessed=12 << 20,
    )(metas, probe_field)
    center, a, b = call(
        update_wide_kernel, (f32(2, EXT, TILE), fold_strip, fold_strip), [SMEM] + [VMEM] * 6
    )(place, center, *sent, *came, scale)
    total, _, came = fold(False, center, swaps((a, b), "col"), RIM)
    return call(
        update_own_kernel, jax.ShapeDtypeStruct((2, TILE, TILE), jnp.float32), [SMEM] + [VMEM] * 5
    )(place, center, total, *came, scale)


def solution(mesh):
    in_specs = (
        P(None, "row", "col"),
        P(),
        P("row", "col", None, None, None),
        P("row", "col", None, None),
        P("row", "col"),
    )
    return jax.shard_map(
        per_device, mesh=mesh, in_specs=in_specs, out_specs=P(None, "row", "col"), check_vma=False
    )
```

```python
import functools
import math

import jax
import jax.numpy as jnp
import numpy as np
from jax import lax
from jax.experimental import pallas as pl
from jax.experimental.pallas import tpu as pltpu
from jax.sharding import PartitionSpec as P

TILE = 256
RIM = 128
MAXPOS = 6
EXT = TILE + 2 * RIM
LANES = 128

smooth_term = 0.25
step_size = 0.5
regular_term = 1.0

VMEM = pl.BlockSpec(memory_space=pltpu.VMEM)
SMEM = pl.BlockSpec(memory_space=pltpu.SMEM)


def dft_tables():
    index = np.arange(TILE)
    angle = (index[:, None] * index[None, :] % TILE) * (2.0 * math.pi / TILE)
    cosine = np.cos(angle) / math.sqrt(TILE)
    sine = -np.sin(angle) / math.sqrt(TILE)
    ahead = np.block([[cosine, -sine], [sine, cosine]]).astype(np.float32)
    return jnp.asarray(np.concatenate([ahead, ahead.T]), jnp.bfloat16)


def swap(value, axis, first):
    count = lax.axis_size(axis)
    pairs = []
    for low in range(first, count - 1, 2):
        pairs += [(low, low + 1), (low + 1, low)]
    return lax.ppermute(value, axis, pairs)


def call(body, out_shapes, in_specs, scratch=(), flops=0, bytes_accessed=1 << 20, vmem=6):
    return pl.pallas_call(
        body,
        out_shape=out_shapes,
        in_specs=in_specs,
        out_specs=jax.tree.map(lambda _: VMEM, out_shapes),
        scratch_shapes=scratch,
        compiler_params=pltpu.CompilerParams(vmem_limit_bytes=vmem << 20),
        cost_estimate=pl.CostEstimate(flops=flops, bytes_accessed=bytes_accessed, transcendentals=0),
    )


def f32(*shape):
    return pltpu.VMEM(shape, jnp.float32)


def aligned(value, unit):
    return pl.multiple_of(value, unit)


def pack_rows_kernel(place, obj, offs, cnt, a_out, b_out):
    parity = place[0] & 1
    a_row = aligned((1 - parity) * RIM, RIM)
    b_row = aligned(parity * RIM, RIM)
    for p in range(2):
        a_out[p * RIM : (p + 1) * RIM, :] = obj[p, pl.ds(a_row, RIM), :]
        b_out[p * RIM : (p + 1) * RIM, :] = obj[p, pl.ds(b_row, RIM), :]
    for out in (a_out, b_out):
        out[2 * RIM :, :] = jnp.zeros((8, TILE), jnp.float32)
        out[2 * RIM : 2 * RIM + 1, 0:12] = offs[...].astype(jnp.float32)
        out[2 * RIM : 2 * RIM + 1, 12:13] = cnt[...].astype(jnp.float32)


def pack_cols_kernel(near, place, obj, row_a, row_b, offs, cnt, out, *meta_out):
    row_odd = place[0] & 1
    a_at = (1 - row_odd) * (RIM + TILE)
    b_at = row_odd * (RIM + TILE)
    high_side = (place[1] & 1) == (0 if near else 1)
    for p in range(2):
        pieces = [(obj[p], p * EXT + RIM, TILE)]
        for row, at in ((row_a, a_at), (row_b, b_at)):
            pieces.append((row[p * RIM : (p + 1) * RIM, :], aligned(p * EXT + at, RIM), RIM))
        for piece, at, size in pieces:
            out[pl.ds(at, size), :] = jnp.where(high_side, piece[:, LANES:TILE], piece[:, 0:LANES])
    meta_a = row_a[2 * RIM : 2 * RIM + 1, 0:LANES]
    meta_b = row_b[2 * RIM : 2 * RIM + 1, 0:LANES]
    odd = row_odd == 1
    meta = out.at[2 * EXT :, :]
    meta[...] = jnp.zeros((8, LANES), jnp.float32)
    meta[0:1, :] = jnp.where(odd, meta_a, meta_b)
    meta[1:2, 0:12] = offs[...].astype(jnp.float32)
    meta[1:2, 12:13] = cnt[...].astype(jnp.float32)
    meta[2:3, :] = jnp.where(odd, meta_b, meta_a)
    for more in meta_out:
        more[...] = meta[...]


def center_kernel(place, obj, row_a, row_b, tables, center):
    row_odd = place[0] & 1
    a_at = aligned((1 - row_odd) * (RIM + TILE), RIM)
    b_at = aligned(row_odd * (RIM + TILE), RIM)
    for p in range(2):
        center[p, RIM : RIM + TILE, :] = obj[p]
        center[p, pl.ds(a_at, RIM), :] = row_a[p * RIM : (p + 1) * RIM, :]
        center[p, pl.ds(b_at, RIM), :] = row_b[p * RIM : (p + 1) * RIM, :]


def light_kernel(metas, probe, out, canvas, padded):
    power = probe[0] * probe[0] + probe[1] * probe[1]
    padded[...] = jnp.zeros_like(padded)
    for b in range(2):
        padded[b + 1] = power[:, b * LANES : (b + 1) * LANES]
    canvas[...] = jnp.zeros_like(canvas)
    lane = lax.broadcasted_iota(jnp.int32, (TILE, LANES), 1)

    def add(index, carry):
        near = index // MAXPOS
        slot = index - near * MAXPOS
        where = (near % 3) * 8 + near // 3
        used = slot < metas[where, 2 * MAXPOS]
        row = (near // 3) * TILE + metas[where, 2 * slot]
        col = (near % 3 - 1) * TILE - RIM + metas[where, 2 * slot + 1]
        for b in range(2):
            start = b * LANES - col

            @pl.when(used & (start > -LANES) & (start < TILE))
            def _():
                spot = start + LANES
                block = spot // LANES
                shift = spot - block * LANES
                back = (LANES - shift) & (LANES - 1)
                first = pltpu.roll(padded[block], back, 1)
                second = pltpu.roll(padded[block + 1], back, 1)
                part = jnp.where(lane < LANES - shift, first, second)
                canvas[b, pl.ds(row, TILE), :] += part

        return carry

    lax.fori_loop(0, 9 * MAXPOS, add, 0)
    for b in range(2):
        out[:, b * LANES : (b + 1) * LANES] = step_size / (
            canvas[b, TILE : TILE + EXT, :] + regular_term
        )


def product(left, right):
    return jnp.dot(left, right, preferred_element_type=jnp.float32)


def transform(table, other, wave):
    half = product(table[...], wave).astype(jnp.bfloat16)
    return product(half[:TILE], other[0:TILE, :]) + product(half[TILE:], other[TILE:, :])


def iterate_kernel(
    first, place, offs, cnt, meta, center, col_a, col_b, probe, amps, tables, own, a_out, b_out, *rest
):
    ext, grad, wave, residual = rest[-4:]
    ahead = tables.at[0 : 2 * TILE]
    back = tables.at[2 * TILE : 4 * TILE]
    if first:
        odd = (place[1] & 1) == 1
        from_a = col_a[2 * EXT :, :]
        from_b = col_b[2 * EXT :, :]
        for side, rows in enumerate((jnp.where(odd, from_a, from_b), meta[...], jnp.where(odd, from_b, from_a))):
            rest[0][8 * side : 8 * side + 8, :] = rows.astype(jnp.int32)
    parity = place[1] & 1
    a_block = 3 * (1 - parity)
    b_block = 3 * parity
    for p in range(2):
        ext[p, a_block, 0:EXT, :] = col_a[p * EXT : (p + 1) * EXT, :]
        ext[p, b_block, 0:EXT, :] = col_b[p * EXT : (p + 1) * EXT, :]
        for b in range(2):
            ext[p, 1 + b, 0:EXT, :] = center[p, :, b * LANES : (b + 1) * LANES]
    grad[...] = jnp.zeros_like(grad)
    lane = lax.broadcasted_iota(jnp.int32, (TILE, LANES), 1)
    slots = range(MAXPOS)
    rows, shifts, blocks = [], [], []
    for slot in slots:
        in_use = slot < cnt[0]
        col = jnp.where(in_use, offs[2 * slot + 1], 0)
        block = col // LANES
        rows.append(pl.ds(jnp.where(in_use, offs[2 * slot], 0), TILE))
        shifts.append(col - block * LANES)
        blocks.append([block, block + 1, jnp.minimum(block + 2, 3)])
    for slot in slots:
        unshift = (LANES - shifts[slot]) & (LANES - 1)
        keep = lane < LANES - shifts[slot]
        window = []
        for p in range(2):
            turned = [pltpu.roll(ext[p, b, rows[slot], :], unshift, 1) for b in blocks[slot]]
            window.append([jnp.where(keep, turned[h], turned[h + 1]) for h in range(2)])
        for h in range(2):
            at = slice(h * LANES, (h + 1) * LANES)
            pr = probe[0, :, at]
            pi = probe[1, :, at]
            re = window[0][h]
            im = window[1][h]
            wave[slot, 0:TILE, at] = (pr * re - pi * im).astype(jnp.bfloat16)
            wave[slot, TILE : 2 * TILE, at] = (pr * im + pi * re).astype(jnp.bfloat16)
    spectra = [transform(ahead, back, wave[slot]) for slot in slots]
    for slot in slots:
        used = jnp.where(slot < cnt[0], 1.0, 0.0)
        sr = spectra[slot][:, :TILE]
        si = spectra[slot][:, TILE:]
        root = lax.rsqrt(sr * sr + si * si + smooth_term)
        factor = (1.0 - amps[slot].astype(jnp.float32) * root) * used
        residual[slot, 0:TILE, :] = (sr * factor).astype(jnp.bfloat16)
        residual[slot, TILE : 2 * TILE, :] = (si * factor).astype(jnp.bfloat16)
    waves = [transform(back, ahead, residual[slot]) for slot in slots]
    for slot in slots:
        pieces = [[], []]
        for h in range(2):
            at = slice(h * LANES, (h + 1) * LANES)
            pr = probe[0, :, at]
            pi = probe[1, :, at]
            br = waves[slot][:, h * LANES : (h + 1) * LANES]
            bi = waves[slot][:, TILE + h * LANES : TILE + (h + 1) * LANES]
            pieces[0].append(pltpu.roll(pr * br + pi * bi, shifts[slot], 1))
            pieces[1].append(pltpu.roll(pr * bi - pi * br, shifts[slot], 1))
        right = lane >= shifts[slot]
        for p in range(2):
            h0, h1 = pieces[p]
            grad[p, blocks[slot][0], rows[slot], :] += jnp.where(right, h0, 0.0)
            grad[p, blocks[slot][1], rows[slot], :] += jnp.where(right, h1, h0)
            grad[p, blocks[slot][2], rows[slot], :] += jnp.where(right, 0.0, h1)
    for p in range(2):
        a_out[p * EXT : (p + 1) * EXT, :] = grad[p, a_block, 0:EXT, :]
        b_out[p * EXT : (p + 1) * EXT, :] = grad[p, b_block, 0:EXT, :]
        for b in range(2):
            own[p, :, b * LANES : (b + 1) * LANES] = grad[p, 1 + b, 0:EXT, :]


def by_side(place, from_a, from_b):
    even = (place[1] & 1) == 0
    return jnp.where(even, from_b, from_a), jnp.where(even, from_a, from_b)


def fold_strips_kernel(depth, place, own, col_a, col_b, a_out, b_out):
    row_parity = place[0] & 1
    for out, end in ((a_out, 1 - row_parity), (b_out, row_parity)):
        at = end * (EXT - depth)
        mine = pl.ds(aligned(at, RIM), depth)
        for p in range(2):
            theirs = pl.ds(aligned(p * EXT + at, RIM), depth)
            left, right = by_side(place, col_a[theirs, :], col_b[theirs, :])
            out[p, :, 0:LANES] = own[p, mine, 0:LANES] + left
            out[p, :, LANES:TILE] = own[p, mine, LANES:TILE] + right


def fold_inner_kernel(place, own, col_a, col_b, total):
    mine = slice(RIM, RIM + TILE)
    for p in range(2):
        theirs = slice(p * EXT + RIM, p * EXT + RIM + TILE)
        left, right = by_side(place, col_a[theirs, :], col_b[theirs, :])
        total[p, :, 0:LANES] = own[p, mine, 0:LANES] + left
        total[p, :, LANES:TILE] = own[p, mine, LANES:TILE] + right


def update_wide_kernel(place, center, sent_a, sent_b, row_a, row_b, scale, fresh, a_out, b_out):
    row_parity = place[0] & 1
    even = (place[1] & 1) == 0
    for sent, came, end in ((sent_a, row_a, 1 - row_parity), (sent_b, row_b, row_parity)):
        rows = pl.ds(aligned(end * TILE, RIM), TILE)
        for p in range(2):
            fresh[p, rows, :] = center[p, rows, :] - scale[rows, :] * (sent[p] + came[p])

    @pl.when(place[0] == 0)
    def _():
        fresh[:, 0:RIM, :] = jnp.zeros((2, RIM, TILE), jnp.float32)

    @pl.when(place[0] == place[2] - 1)
    def _():
        fresh[:, EXT - RIM :, :] = jnp.zeros((2, RIM, TILE), jnp.float32)

    for p in range(2):
        low = fresh[p, :, 0:LANES]
        high = fresh[p, :, LANES:TILE]
        a_out[p * EXT : (p + 1) * EXT, :] = jnp.where(even, high, low)
        b_out[p * EXT : (p + 1) * EXT, :] = jnp.where(even, low, high)


def update_own_kernel(place, center, total, row_a, row_b, scale, out, fresh, left):
    odd = (place[0] & 1) == 1
    copies = []
    for p in range(2):
        top = jnp.where(odd, row_a[p], row_b[p])
        bottom = jnp.where(odd, row_b[p], row_a[p])
        for half, came in ((0, top), (1, bottom)):
            at = slice(RIM + half * RIM, RIM + (half + 1) * RIM)
            rows = slice(half * RIM, (half + 1) * RIM)
            fresh[p, rows, :] = center[p, at, :] - scale[at, :] * (total[p, rows, :] + came)
            copies.append(
                pltpu.make_async_copy(fresh.at[p, rows, :], out.at[p, rows, :], left.at[len(copies)])
            )
            copies[-1].start()
    for copy in copies:
        copy.wait()


def swaps(values, axis):
    far = swap(values[1], axis, 1)
    return swap(values[0], axis, 0), far


def per_device(object_field, probe_field, amplitudes, offsets, counts):
    tables = dft_tables()
    place = jnp.stack(
        [lax.axis_index("row"), lax.axis_index("col"), lax.axis_size("row"), lax.axis_size("col")]
    ).astype(jnp.int32)
    offs = offsets.reshape(1, 2 * MAXPOS)
    cnt = counts.reshape(1, 1)
    flat_offs = offsets.reshape(2 * MAXPOS)
    flat_cnt = counts.reshape(1)
    amps = amplitudes.reshape(MAXPOS, TILE, TILE)

    row_strip = f32(2 * RIM + 8, TILE)
    strips = call(pack_rows_kernel, (row_strip, row_strip), [SMEM, VMEM, VMEM, VMEM])(
        place, object_field, offs, cnt
    )
    row_a, row_b = swaps(strips, "row")
    col_strip = f32(2 * EXT + 8, LANES)
    def pack_cols(near, *more):
        return call(
            functools.partial(pack_cols_kernel, near), (col_strip,) + more, [SMEM] + [VMEM] * 5
        )(place, object_field, row_a, row_b, offs, cnt)

    (a,) = pack_cols(True)
    b, meta = pack_cols(False, f32(8, LANES))
    center = call(center_kernel, f32(2, EXT, TILE), [SMEM] + [VMEM] * 4, bytes_accessed=4 << 20)(
        place, object_field, row_a, row_b, tables
    )
    col_a, col_b = swaps((a, b), "col")

    fold_strip = f32(2 * EXT, LANES)
    grid = pltpu.VMEM((2, 4, EXT + 8, LANES), jnp.float32)
    stack = pltpu.VMEM((MAXPOS, 2 * TILE, TILE), jnp.bfloat16)

    def iterate(first, center, cols):
        outs = (f32(2, EXT, TILE), fold_strip, fold_strip)
        if first:
            outs += (jax.ShapeDtypeStruct((24, LANES), jnp.int32),)
        return call(
            functools.partial(iterate_kernel, first),
            outs,
            [SMEM] * 3 + [VMEM] * 7,
            [grid, grid, stack, stack],
            flops=3 << 30,
            bytes_accessed=6 << 20,
            vmem=14,
        )(place, flat_offs, flat_cnt, meta, center, *cols, probe_field, amps, tables)

    def fold(first, center, cols, depth):
        own, a, b, *metas = iterate(first, center, cols)
        a, b = swaps((a, b), "col")
        sent = call(
            functools.partial(fold_strips_kernel, depth),
            (f32(2, depth, TILE), f32(2, depth, TILE)),
            [SMEM] + [VMEM] * 3,
        )(place, own, a, b)
        came = swaps(sent, "row")
        if first:
            return sent, metas[0], came
        total = call(fold_inner_kernel, f32(2, TILE, TILE), [SMEM] + [VMEM] * 3, bytes_accessed=4 << 20)(
            place, own, a, b
        )
        return total, None, came

    sent, metas, came = fold(True, center, (col_a, col_b), TILE)
    scale = call(
        light_kernel,
        f32(EXT, TILE),
        [SMEM, VMEM],
        [pltpu.VMEM((2, 4 * TILE + 8, LANES), jnp.float32), pltpu.VMEM((5, TILE, LANES), jnp.float32)],
        bytes_accessed=12 << 20,
    )(metas, probe_field)
    center, a, b = call(
        update_wide_kernel, (f32(2, EXT, TILE), fold_strip, fold_strip), [SMEM] + [VMEM] * 6
    )(place, center, *sent, *came, scale)
    total, _, came = fold(False, center, swaps((a, b), "col"), RIM)
    return pl.pallas_call(
        update_own_kernel,
        out_shape=jax.ShapeDtypeStruct((2, TILE, TILE), jnp.float32),
        in_specs=[SMEM] + [VMEM] * 5,
        out_specs=pl.BlockSpec(memory_space=pl.ANY),
        scratch_shapes=[pltpu.VMEM((2, TILE, TILE), jnp.float32), pltpu.SemaphoreType.DMA((4,))],
        compiler_params=pltpu.CompilerParams(vmem_limit_bytes=6 << 20),
    )(place, center, total, *came, scale)


def solution(mesh):
    in_specs = (
        P(None, "row", "col"),
        P(),
        P("row", "col", None, None, None),
        P("row", "col", None, None),
        P("row", "col"),
    )
    return jax.shard_map(
        per_device, mesh=mesh, in_specs=in_specs, out_specs=P(None, "row", "col"), check_vma=False
    )
```
